256 devices in a mesh: pool: 32 (over z_lo, y, core), tensor: 8 (over x, z_hi).
Axes of the slice: x: 4, y: 4, z: 8 (z_hi: 2, z_lo: 4; z = z_hi * 4 + z_lo), core: 2. Of those that a mesh axis runs over, the one named last changes fastest.
Arguments:
- queries: bfloat16 [512, 8192], P('pool', 'tensor'), may hold values from -6 to 6
- cache_keys: bfloat16 [512, 256, 1024], P('pool', None, 'tensor'), may hold values from -6 to 6
- cache_values: bfloat16 [512, 256, 1024], P('pool', None, 'tensor'), may hold values from -6 to 6
- context_lens: int32 [512], P('pool'), may hold values from 2 to 256
- prompt_keys: bfloat16 [1024, 32, 1024], P('pool', None, 'tensor'), may hold values from -6 to 6
- prompt_values: bfloat16 [1024, 32, 1024], P('pool', None, 'tensor'), may hold values from -6 to 6
- prompt_lens: int32 [1024], P('pool'), may hold values from 1 to 32
- matching: int32 [1024, 1], P('pool'), may hold values from 0 to 31; in each aligned block of 32 rows (0 to 31, 32 to 63, ...) at most 2 rows name the same one
- dest_seq: int32 [1024], P('pool'), may hold values from 0 to 15
- out_weight: bfloat16 [8192, 4096], P('tensor'), may hold values from -0.5 to 0.5
Outputs:
- projected: bfloat16 [512, 4096], P('pool', 'tensor')
The draws below stay inside these ranges and needn't reach their ends.
Inputs may be any that keep to these rules, and one draw needn't show every extreme that they name: `matching`: among the 32 prompts of one group at most 2 name the same receiving group, and in some group exactly 2 do.
All inputs are finite; a program needn't handle non-finite values.
Results may differ from the reference program's by a relative error of at most 0.017.
Values may be sent and summed in bfloat16 or wider, within the bound.
No kernel may reach another device: no remote copies, remote signals or barrier semaphores. Data moves between devices by JAX's collectives and lax.ppermute only.
A program may use at most 128 MiB of HBM per device.

```python
import math
import jax
import jax.numpy as jnp
import numpy as np
from jax import lax

HQ = 64
KVH = 8
HD = 128
D_OUT = 4096
SEQ_DEV = 16
CTX = 256
PR_DEV = 32
PLEN = 32
CAP = 2
SEQS = 512
PROMPTS = 1024
N_POOL = 32


def draw_queries(key, part):
    key = jax.random.fold_in(key, 1)
    values = jnp.clip(2.0 * jax.random.normal(key, (SEQS, KVH, HQ // KVH, HD), jnp.float32), -6.0, 6.0)
    return values.reshape(SEQS, HQ * HD).astype(jnp.bfloat16)


def draw_cache_keys(key, part):
    key = jax.random.fold_in(key, 2)
    values = jnp.clip(jax.random.normal(key, (SEQS, CTX, KVH, HD), jnp.float32), -6.0, 6.0)
    return values.reshape(SEQS, CTX, KVH * HD).astype(jnp.bfloat16)


def touch_ends(drawn, key, least, top_value):
    longest = drawn.shape.index(max(drawn.shape))
    spots = []
    for shift in (0, 1):
        where = [jax.random.randint(jax.random.fold_in(key, axis), (), 0, length) for axis, length in enumerate(drawn.shape)]
        where[longest] = (where[longest] + shift) % drawn.shape[longest]
        spots.append(tuple(where))
    return drawn.at[spots[0]].set(least).at[spots[1]].set(top_value)


def level_of(own_key, shape, pieces, smallest, largest):
    factor_of, own = 1.0, jax.random.fold_in(own_key, 6)
    for dim, shards_of in pieces:
        draws = jnp.exp(jax.random.uniform(jax.random.fold_in(own, dim), (shards_of,), jnp.float32, smallest / len(pieces), largest / len(pieces)))
        factor_of = factor_of * jnp.repeat(draws, shape[dim] // shards_of).reshape([-1 if axis == dim else 1 for axis in range(len(shape))])
    return factor_of


def deal_out(own_key, own, number, rows, count, top, limit, slope):
    ranking = jax.random.permutation(own_key, count)
    crowded, usual = load_shares(count, rows * top, limit, slope, True), load_shares(count, rows * top, limit, slope, False)
    places = jnp.arange(count)

    def named(tallies, rotation):
        used = int((tallies > 0).sum())
        fixed = max(1, used // 4)
        shifted = fixed + (places - fixed + rotation * (used - fixed)) % max(1, count - fixed)
        return jnp.zeros((count,), jnp.int32).at[ranking[jnp.where(places < fixed, places, shifted)]].set(jnp.asarray(tallies, jnp.int32))

    tallies = jnp.where(number % 4 == 0, named(crowded, number // 4), named(usual, number - number // 4 - 1))
    mixed = jax.random.permutation(jax.random.fold_in(own, 3), count)
    donor, taker = mixed[0:count // 2 * 2:2], mixed[1:count // 2 * 2:2]
    room = jnp.minimum(tallies[donor] - 1, limit - tallies[taker]) // 2
    room = jnp.where((donor == ranking[0]) | (taker == ranking[0]) | (tallies[taker] == 0), 0, jnp.maximum(room, 0))
    shifted = jax.random.randint(jax.random.fold_in(own, 4), (count // 2,), 0, 1 << 20) % (room + 1)
    tallies = tallies.at[donor].add(-shifted).at[taker].add(shifted)
    labels = jnp.searchsorted(jnp.cumsum(tallies), jnp.arange(rows * top), side="right").astype(jnp.int32)
    grid = labels.reshape(top, rows).T
    grid = grid[jax.random.permutation(jax.random.fold_in(own, 1), rows)]
    rotation = jax.random.randint(jax.random.fold_in(own, 2), (rows, 1), 0, top)
    return jnp.take_along_axis(grid, (jnp.arange(top)[None, :] + rotation) % top, axis=1)


def load_shares(count, total, reach, slope, full):
    loads = [(1 << 20) // math.isqrt(rank ** slope) + 1 for rank in range(1, count + 1)]
    largest = reach if full else min(reach, max(-(-total // count), total * loads[0] // sum(loads)))
    least = 1 if total - largest >= count - 1 else 0
    holding, spare = [largest] + [least] * (count - 1), total - largest - least * (count - 1)
    while spare > 0:
        free = [i for i in range(1, count) if holding[i] < largest] or [i for i in range(1, count) if holding[i] < reach]
        pool, left = sum([loads[i] for i in free]), spare
        for i in free:
            extra = min(reach - holding[i], max(1, left * loads[i] // pool), spare)
            holding[i] = holding[i] + extra
            spare = spare - extra
    return np.array(holding)


def noise(stream_key, dims, deviation, reach, cuts=(), dtype=jnp.bfloat16):
    array = deviation * jax.random.normal(stream_key, dims, jnp.float32)
    if cuts:
        array = array * level_of(stream_key, dims, cuts, -0.22, 0.18)
    return jnp.clip(array, -reach, reach).astype(dtype)


def setup_inputs(seed: int = 0) -> dict:
    keys = jax.random.split(jax.random.key(seed), 11)
    queries = draw_queries(jax.random.fold_in(keys[10], 71), 0)
    cache_keys = draw_cache_keys(jax.random.fold_in(keys[10], 71), 0)
    cache_values = noise(keys[2], (SEQS, CTX, KVH * HD), 1.0, 6.0, ((0, 32), (2, 8)))
    context_lens = touch_ends(jax.random.randint(keys[3], (SEQS,), 2, CTX + 1), jax.random.fold_in(keys[3], 1), 2, CTX).astype(jnp.int32)
    prompt_keys = noise(keys[4], (PROMPTS, PLEN, KVH * HD), 1.0, 6.0, ((0, 32), (2, 8)))
    prompt_values = noise(keys[5], (PROMPTS, PLEN, KVH * HD), 1.0, 6.0, ((0, 32), (2, 8)))
    prompt_lens = touch_ends(jax.random.randint(keys[6], (PROMPTS,), 1, PLEN + 1), jax.random.fold_in(keys[6], 1), 1, PLEN).astype(jnp.int32)
    matching_keys = jax.random.split(jax.random.fold_in(keys[7], 1), PROMPTS // PR_DEV)
    matching_turns = jax.random.permutation(jax.random.fold_in(keys[7], 3), PROMPTS // PR_DEV)
    matching = jax.vmap(lambda own, number: deal_out(jax.random.fold_in(keys[7], 2), own, number, PR_DEV, N_POOL, 1, CAP, 2))(matching_keys, matching_turns).reshape((PROMPTS, 1))
    dest_seq = touch_ends(jax.random.randint(keys[8], (PROMPTS,), 0, SEQ_DEV), jax.random.fold_in(keys[8], 1), 0, SEQ_DEV - 1).astype(jnp.int32)
    out_weight = noise(keys[9], (HQ * HD, D_OUT), HD ** -0.5, 0.5, ((0, 8),))
    return {"queries": queries, "cache_keys": cache_keys, "cache_values": cache_values, "context_lens": context_lens, "prompt_keys": prompt_keys, "prompt_values": prompt_values, "prompt_lens": prompt_lens, "matching": matching, "dest_seq": dest_seq, "out_weight": out_weight}


def reference(queries, cache_keys, cache_values, context_lens, prompt_keys, prompt_values, prompt_lens, matching, dest_seq, out_weight):
    repeat = HQ // KVH
    score_scale = 1.0 / math.sqrt(HD)
    query_heads = queries.astype(jnp.float32).reshape(SEQS, KVH, repeat, HD)
    cache_k = cache_keys.astype(jnp.float32).reshape(SEQS, CTX, KVH, HD)
    cache_v = cache_values.astype(jnp.float32).reshape(SEQS, CTX, KVH, HD)
    cache_scores = jnp.einsum('sgrd,scgd->sgrc', query_heads, cache_k) * score_scale
    cache_alive = jnp.arange(CTX)[None, :] < context_lens[:, None]
    cache_scores = jnp.where(cache_alive[:, None, None, :], cache_scores, -jnp.inf)
    target = (matching[:, 0] * SEQ_DEV + dest_seq).astype(jnp.int32)
    prompt_q = query_heads[target]
    prompt_k = prompt_keys.astype(jnp.float32).reshape(PROMPTS, PLEN, KVH, HD)
    prompt_v = prompt_values.astype(jnp.float32).reshape(PROMPTS, PLEN, KVH, HD)
    prompt_scores = jnp.einsum('pgrd,ptgd->pgrt', prompt_q, prompt_k) * score_scale
    prompt_alive = jnp.arange(PLEN)[None, :] < prompt_lens[:, None]
    prompt_scores = jnp.where(prompt_alive[:, None, None, :], prompt_scores, -jnp.inf)
    prompt_top = lax.optimization_barrier(jnp.max(prompt_scores, axis=-1))
    belongs = target[None, :] == jnp.arange(SEQS)[:, None]
    joined_top = lax.optimization_barrier(jnp.max(jnp.where(belongs[:, :, None, None], prompt_top[None], -jnp.inf), axis=1))
    row_top = jnp.maximum(lax.optimization_barrier(jnp.max(cache_scores, axis=-1)), joined_top)
    cache_exp = jnp.exp(cache_scores - row_top[..., None])
    prompt_exp = jnp.exp(prompt_scores - row_top[target][..., None])
    denominator = lax.optimization_barrier(jnp.sum(cache_exp, axis=-1)) + jax.ops.segment_sum(lax.optimization_barrier(jnp.sum(prompt_exp, axis=-1)), target, num_segments=SEQS)
    cache_weights = lax.optimization_barrier(cache_exp.astype(jnp.bfloat16)).astype(jnp.float32)
    prompt_weights = lax.optimization_barrier(prompt_exp.astype(jnp.bfloat16)).astype(jnp.float32)
    weighted = jnp.einsum('sgrc,scgd->sgrd', cache_weights, cache_v)
    weighted = weighted + jax.ops.segment_sum(jnp.einsum('pgrt,ptgd->pgrd', prompt_weights, prompt_v), target, num_segments=SEQS)
    attended = (weighted / denominator[..., None]).astype(jnp.bfloat16).reshape(SEQS, HQ * HD)
    return jnp.dot(attended, out_weight, preferred_element_type=jnp.float32).astype(jnp.bfloat16)
```

```python
import functools
import math

import jax
import jax.numpy as jnp
from jax import lax
from jax.experimental import pallas as pl
from jax.experimental.pallas import tpu as pltpu
from jax.sharding import PartitionSpec as P

HD = 128
CAP = 2
NEG = -(2.0**99)
VMEM = pltpu.VMEM
SMEM = pltpu.SMEM
NT = (((1,), (1,)), ((), ()))


def pack_kernel(half, owner_ref, dest_ref, len_ref, keys_ref, values_ref, out_ref, count, index, length, target):
    prompts, plen, _ = keys_ref.shape
    blocks = out_ref.shape[0]
    width = CAP * plen
    my_half = lax.axis_index("pool") // half
    for i in range(2 * half):
        count[i] = 0
    for i in range(blocks * 2 * CAP):
        index[i] = 0
        length[i] = 0
        target[i] = 0
    for p in range(prompts):
        group = owner_ref[p, 0]
        rank = count[group]
        count[group] = rank + 1
        other = jnp.where(group // half == my_half, 0, 1)
        slot = (group % half) * (2 * CAP) + other * CAP + jnp.minimum(rank, CAP - 1)
        index[slot] = p
        length[slot] = len_ref[p]
        target[slot] = dest_ref[p]
    row = lax.broadcasted_iota(jnp.int32, (16, 128), 0)
    lane = lax.broadcasted_iota(jnp.int32, (16, 128), 1)
    pos = lane % plen
    second = (lane // plen) % CAP == 1
    lower = row < 8
    for b in range(blocks):
        for other in range(2):
            for r in range(CAP):
                p = index[b * 2 * CAP + other * CAP + r]
                at = other * 2 * width + r * plen
                out_ref[b, at : at + plen, :] = keys_ref[p]
                out_ref[b, at + width : at + width + plen, :] = values_ref[p]
        s = b * 2 * CAP
        limit = jnp.where(
            lower,
            jnp.where(second, length[s + 1], length[s]),
            jnp.where(second, length[s + 3], length[s + 2]),
        )
        code = jnp.where(
            lower,
            jnp.where(second, target[s + 1], target[s]),
            jnp.where(second, target[s + 3], target[s + 2]),
        )
        code = jnp.where(pos < limit, code, -1)
        out_ref[b, 4 * width :, :] = code.astype(jnp.float32).astype(jnp.bfloat16)


def split_heads(q_ref, scratch):
    seqs = q_ref.shape[0]
    heads = q_ref.shape[1] // HD
    for h in range(heads):
        scratch[h * seqs : (h + 1) * seqs, :] = q_ref[:, h * HD : (h + 1) * HD].astype(jnp.float32)
    return [scratch[pl.ds(s, heads, stride=seqs), :] for s in range(seqs)]


def prompt_scores(q, got_ref, other, scale):
    blocks, rows, _ = got_ref.shape
    width = (rows - 16) // 4
    at = other * 2 * width
    seq = lax.broadcasted_iota(jnp.int32, (q.shape[0], 128), 0) // 8
    left = lax.broadcasted_iota(jnp.int32, (8, 128), 1) < width
    out = []
    for b in range(0, blocks, 2):
        keys = jnp.concatenate([got_ref[b, at : at + width, :], got_ref[b + 1, at : at + width, :]], axis=0)
        s = lax.dot_general(q, keys, NT, preferred_element_type=jnp.float32) * scale
        meta0 = got_ref[b, 4 * width :, :].astype(jnp.float32)
        meta1 = got_ref[b + 1, 4 * width :, :].astype(jnp.float32)
        code = jnp.where(left, meta0[other * 8 : other * 8 + 8], meta1[other * 8 : other * 8 + 8])[0:1]
        out.append(jnp.where(seq == code.astype(jnp.int32), s, NEG))
    return out


def prompt_sum(weights, got_ref, other):
    blocks, rows, _ = got_ref.shape
    width = (rows - 16) // 4
    at = other * 2 * width + width
    total = None
    for i, b in enumerate(range(0, blocks, 2)):
        values = jnp.concatenate([got_ref[b, at : at + width, :], got_ref[b + 1, at : at + width, :]], axis=0)
        part = jnp.dot(weights[i].astype(jnp.bfloat16), values, preferred_element_type=jnp.float32)
        total = part if total is None else total + part
    return total


def partner_kernel(scale, q_ref, got_ref, out_ref, scratch):
    q = jnp.concatenate(split_heads(q_ref, scratch), axis=0).astype(jnp.bfloat16)
    scores = prompt_scores(q, got_ref, 1, scale)
    top = functools.reduce(jnp.maximum, scores)
    top = jnp.max(top, axis=1, keepdims=True).astype(jnp.bfloat16).astype(jnp.float32)
    exps = [jnp.exp(s - top) for s in scores]
    total = jnp.sum(functools.reduce(jnp.add, exps), axis=1, keepdims=True)
    rows = q.shape[0]
    out_ref[:rows, :] = prompt_sum(exps, got_ref, 1).astype(jnp.bfloat16)
    high = total.astype(jnp.bfloat16).astype(jnp.float32)
    lane = lax.broadcasted_iota(jnp.int32, (rows, 128), 1)
    stats = jnp.where(lane == 0, top, jnp.where(lane == 1, high, total - high))
    out_ref[rows:, :] = jnp.transpose(stats)[:16, :].astype(jnp.bfloat16)


def main_kernel(scale, lens_ref, q_ref, keys_ref, values_ref, got_ref, out_ref, top_ref, sum_ref, scratch):
    seqs, ctx, _ = keys_ref.shape
    rows = split_heads(q_ref, scratch)
    q = jnp.concatenate(rows, axis=0).astype(jnp.bfloat16)
    heads = q.shape[0] // seqs
    col = lax.broadcasted_iota(jnp.int32, (heads, ctx), 1)
    cache = []
    for s in range(seqs):
        sc = lax.dot_general(rows[s].astype(jnp.bfloat16), keys_ref[s], NT, preferred_element_type=jnp.float32)
        cache.append(jnp.where(col < lens_ref[s], sc * scale, NEG))
    scores = prompt_scores(q, got_ref, 0, scale)
    cache_all = jnp.concatenate(cache, axis=0)
    top = functools.reduce(jnp.maximum, scores + [cache_all[:, i : i + 128] for i in range(0, ctx, 128)])
    top = jnp.max(top, axis=1, keepdims=True)
    cache_exp = jnp.exp(cache_all - top)
    exps = [jnp.exp(s - top) for s in scores]
    total = functools.reduce(jnp.add, exps + [cache_exp[:, i : i + 128] for i in range(0, ctx, 128)])
    total = jnp.sum(total, axis=1, keepdims=True)
    parts = []
    for s in range(seqs):
        w = cache_exp[s * heads : (s + 1) * heads].astype(jnp.bfloat16)
        parts.append(jnp.dot(w, values_ref[s], preferred_element_type=jnp.float32))
    out_ref[...] = jnp.concatenate(parts, axis=0) + prompt_sum(exps, got_ref, 0)
    top_ref[...] = jnp.broadcast_to(top, top_ref.shape)
    sum_ref[...] = jnp.broadcast_to(total, sum_ref.shape)


def project_kernel(main_ref, top_ref, sum_ref, back_ref, weight_ref, out_ref, scratch):
    pieces, seqs, cols = out_ref.shape
    rows = main_ref.shape[0]
    heads = rows // seqs
    stats = jnp.concatenate([back_ref[rows:, :].astype(jnp.float32)] * (128 // 16), axis=0)
    stats = jnp.transpose(stats)
    far_top = stats[:, 0:1]
    far_sum = stats[:, 1:2] + stats[:, 2:3]
    top = jnp.maximum(top_ref[...], far_top)
    near = jnp.exp(top_ref[...] - top)
    far = jnp.exp(far_top - top)
    total = sum_ref[...] * near + far_sum * far
    scratch[...] = (main_ref[...] * near + back_ref[:rows, :].astype(jnp.float32) * far) / total
    attended = jnp.concatenate(
        [scratch[pl.ds(h, seqs, stride=heads), :].astype(jnp.bfloat16) for h in range(heads)], axis=1
    )
    for c in range(pieces):
        part = jnp.dot(attended, weight_ref[:, c * cols : (c + 1) * cols], preferred_element_type=jnp.float32)
        out_ref[c] = part.astype(out_ref.dtype)


def vmem(n):
    return [pl.BlockSpec(memory_space=VMEM)] * n


def smem(n):
    return [pl.BlockSpec(memory_space=SMEM)] * n


def shards(
    queries,
    cache_keys,
    cache_values,
    context_lens,
    prompt_keys,
    prompt_values,
    prompt_lens,
    matching,
    dest_seq,
    out_weight,
):
    seqs, q_width = queries.shape
    ctx = cache_keys.shape[1]
    prompts, plen, _ = prompt_keys.shape
    pool = lax.axis_size("pool")
    pieces = lax.axis_size("tensor")
    out_cols = out_weight.shape[1]
    half = pool // 2
    rows = q_width // HD * seqs
    width = CAP * plen
    scale = 1.0 / math.sqrt(HD)
    swap = [(i, (i + half) % pool) for i in range(pool)]
    halves = [list(range(half)), list(range(half, pool))]
    far_queries = lax.ppermute(queries, "pool", swap)
    packed = pl.pallas_call(
        functools.partial(pack_kernel, half),
        out_shape=jax.ShapeDtypeStruct((half, 4 * width + 16, HD), jnp.bfloat16),
        in_specs=smem(3) + vmem(2),
        out_specs=pl.BlockSpec(memory_space=VMEM),
        scratch_shapes=[
            SMEM((pool,), jnp.int32),
            SMEM((half * 2 * CAP,), jnp.int32),
            SMEM((half * 2 * CAP,), jnp.int32),
            SMEM((half * 2 * CAP,), jnp.int32),
        ],
        name="pack",
    )(matching, dest_seq, prompt_lens, prompt_keys, prompt_values)
    got = lax.all_to_all(packed, "pool", 0, 0, axis_index_groups=halves)
    back = pl.pallas_call(
        functools.partial(partner_kernel, scale),
        out_shape=jax.ShapeDtypeStruct((rows + 16, HD), jnp.bfloat16),
        in_specs=vmem(2),
        out_specs=pl.BlockSpec(memory_space=VMEM),
        scratch_shapes=[VMEM((rows, HD), jnp.float32)],
        compiler_params=pltpu.CompilerParams(vmem_limit_bytes=16 << 20),
        name="partner",
    )(far_queries, got)
    back = lax.ppermute(back, "pool", swap)
    main, top, total = pl.pallas_call(
        functools.partial(main_kernel, scale),
        out_shape=[jax.ShapeDtypeStruct((rows, HD), jnp.float32)] * 3,
        in_specs=smem(1) + vmem(4),
        out_specs=vmem(3),
        scratch_shapes=[VMEM((rows, HD), jnp.float32)],
        compiler_params=pltpu.CompilerParams(vmem_limit_bytes=24 << 20),
        cost_estimate=pl.CostEstimate(flops=200_000_000, bytes_accessed=4_000_000, transcendentals=200_000),
        name="main",
    )(context_lens, queries, cache_keys, cache_values, got)
    parts = pl.pallas_call(
        project_kernel,
        out_shape=jax.ShapeDtypeStruct((pieces, seqs, out_cols // pieces), jnp.bfloat16),
        in_specs=vmem(5),
        out_specs=pl.BlockSpec(memory_space=VMEM),
        scratch_shapes=[VMEM((rows, HD), jnp.float32)],
        compiler_params=pltpu.CompilerParams(vmem_limit_bytes=24 << 20),
        name="project",
    )(main, top, total, back, out_weight)
    parts = lax.all_to_all(parts, "tensor", 0, 0)
    return jnp.sum(parts.astype(jnp.float32), axis=0).astype(jnp.bfloat16)


def solution(mesh):
    placed = (
        P("pool", "tensor"),
        P("pool", None, "tensor"),
        P("pool", None, "tensor"),
        P("pool"),
        P("pool", None, "tensor"),
        P("pool", None, "tensor"),
        P("pool"),
        P("pool", None),
        P("pool"),
        P("tensor", None),
    )
    return jax.shard_map(
        shards, mesh=mesh, in_specs=placed, out_specs=P("pool", "tensor"), check_vma=False
    )
```

```python
import functools
import math

import jax
import jax.numpy as jnp
from jax import lax
from jax.experimental import pallas as pl
from jax.experimental.pallas import tpu as pltpu
from jax.sharding import PartitionSpec as P

HD = 128
CAP = 2
EARLY = 256
LATE = 0
NEG = -(2.0**99)
VMEM = pltpu.VMEM
SMEM = pltpu.SMEM
NT = (((1,), (1,)), ((), ()))


def pack_kernel(
    half, owner_hbm, dest_hbm, len_hbm, keys_hbm, values_hbm, out_ref, owner_ref, dest_ref, len_ref, keys, values, sems, count, length, target
):
    prompts, plen, _ = keys.shape
    blocks = out_ref.shape[0]
    width = CAP * plen
    pairs = ((owner_hbm, owner_ref), (dest_hbm, dest_ref), (len_hbm, len_ref), (keys_hbm, keys), (values_hbm, values))
    loads = [pltpu.make_async_copy(a, b, sems.at[i]) for i, (a, b) in enumerate(pairs)]
    for load in loads:
        load.start()
    zeros = jnp.zeros((width, HD), jnp.bfloat16)
    for b in range(blocks):
        out_ref[b, width : 2 * width, :] = zeros
        out_ref[b, 3 * width : 4 * width, :] = zeros
    my_half = lax.axis_index("pool") // half
    for i in range(2 * half):
        count[i] = 0
    for i in range(blocks * 2 * CAP):
        length[i] = 0
        target[i] = 0
    for load in loads[:3]:
        load.wait()
    places = []
    for p in range(prompts):
        group = owner_ref[p]
        rank = jnp.minimum(count[group], CAP - 1)
        count[group] = rank + 1
        block = group % half
        other = jnp.where(group // half == my_half, 0, 1)
        slot = block * (2 * CAP) + other * CAP + rank
        length[slot] = len_ref[p]
        target[slot] = dest_ref[p]
        places.append((block, other * 2 * width + rank * plen))
    row = lax.broadcasted_iota(jnp.int32, (16, 128), 0)
    lane = lax.broadcasted_iota(jnp.int32, (16, 128), 1)
    pos = lane % plen
    second = (lane // plen) % CAP == 1
    lower = row < 8
    for b in range(blocks):
        s = b * 2 * CAP
        limit = jnp.where(
            lower,
            jnp.where(second, length[s + 1], length[s]),
            jnp.where(second, length[s + 3], length[s + 2]),
        )
        code = jnp.where(
            lower,
            jnp.where(second, target[s + 1], target[s]),
            jnp.where(second, target[s + 3], target[s + 2]),
        )
        code = jnp.where(pos < limit, code, -1)
        out_ref[b, 4 * width :, :] = code.astype(jnp.float32).astype(jnp.bfloat16)
    for load in loads[3:]:
        load.wait()
    for p, (block, at) in enumerate(places):
        out_ref[block, pl.ds(pl.multiple_of(at, plen), plen), :] = keys[p]
        out_ref[block, pl.ds(pl.multiple_of(at + width, plen), plen), :] = values[p]


def split_heads(q_ref, scratch):
    seqs = q_ref.shape[0]
    heads = q_ref.shape[1] // HD
    for h in range(heads):
        scratch[h * seqs : (h + 1) * seqs, :] = q_ref[:, h * HD : (h + 1) * HD].astype(jnp.float32)
    return [scratch[pl.ds(s, heads, stride=seqs), :] for s in range(seqs)]


def prompt_scores(q, got_ref, other, scale):
    blocks, rows, _ = got_ref.shape
    width = (rows - 16) // 4
    at = other * 2 * width
    seq = lax.broadcasted_iota(jnp.int32, (q.shape[0], 128), 0) // 8
    left = lax.broadcasted_iota(jnp.int32, (8, 128), 1) < width
    out = []
    for b in range(0, blocks, 2):
        keys = jnp.concatenate([got_ref[b, at : at + width, :], got_ref[b + 1, at : at + width, :]], axis=0)
        s = lax.dot_general(q, keys, NT, preferred_element_type=jnp.float32) * scale
        meta0 = got_ref[b, 4 * width :, :].astype(jnp.float32)
        meta1 = got_ref[b + 1, 4 * width :, :].astype(jnp.float32)
        code = jnp.where(left, meta0[other * 8 : other * 8 + 8], meta1[other * 8 : other * 8 + 8])[0:1]
        out.append(jnp.where(seq == code.astype(jnp.int32), s, NEG))
    return out


def prompt_sum(weights, got_ref, other):
    blocks, rows, _ = got_ref.shape
    width = (rows - 16) // 4
    at = other * 2 * width + width
    total = None
    for i, b in enumerate(range(0, blocks, 2)):
        values = jnp.concatenate([got_ref[b, at : at + width, :], got_ref[b + 1, at : at + width, :]], axis=0)
        part = jnp.dot(weights[i].astype(jnp.bfloat16), values, preferred_element_type=jnp.float32)
        total = part if total is None else total + part
    return total


def partner_kernel(scale, q_ref, got_ref, out_ref, scratch):
    q = jnp.concatenate(split_heads(q_ref, scratch), axis=0).astype(jnp.bfloat16)
    scores = prompt_scores(q, got_ref, 1, scale)
    top = functools.reduce(jnp.maximum, scores)
    top = jnp.max(top, axis=1, keepdims=True).astype(jnp.bfloat16).astype(jnp.float32)
    exps = [jnp.exp(s - top) for s in scores]
    total = jnp.sum(functools.reduce(jnp.add, exps), axis=1, keepdims=True)
    rows = q.shape[0]
    out_ref[:rows, :] = prompt_sum(exps, got_ref, 1).astype(jnp.bfloat16)
    high = total.astype(jnp.bfloat16).astype(jnp.float32)
    lane = lax.broadcasted_iota(jnp.int32, (rows, 128), 1)
    stats = jnp.where(lane == 0, top, jnp.where(lane == 1, high, total - high))
    out_ref[rows:, :] = jnp.transpose(stats)[:16, :].astype(jnp.bfloat16)


def cache_kernel(scale, lens_ref, q_ref, keys_ref, values_ref, weight_hbm, out_ref, top_ref, sum_ref, q_out_ref, weight_ref, scratch, sem):
    load = pltpu.make_async_copy(weight_hbm.at[:EARLY], weight_ref, sem)
    load.start()
    seqs, ctx, _ = keys_ref.shape
    rows = split_heads(q_ref, scratch)
    q_out_ref[...] = jnp.concatenate(rows, axis=0)
    heads = rows[0].shape[0]
    col = lax.broadcasted_iota(jnp.int32, (heads, ctx), 1)
    scores = []
    for s in range(seqs):
        sc = lax.dot_general(rows[s].astype(jnp.bfloat16), keys_ref[s], NT, preferred_element_type=jnp.float32)
        scores.append(jnp.where(col < lens_ref[s], sc * scale, NEG))
    scores = jnp.concatenate(scores, axis=0)
    top = jnp.max(scores, axis=1, keepdims=True)
    exps = jnp.exp(scores - top)
    total = jnp.sum(exps, axis=1, keepdims=True)
    for s in range(seqs):
        w = exps[s * heads : (s + 1) * heads].astype(jnp.bfloat16)
        out_ref[s * heads : (s + 1) * heads, :] = jnp.dot(w, values_ref[s], preferred_element_type=jnp.float32)
    top_ref[...] = jnp.broadcast_to(top, top_ref.shape)
    sum_ref[...] = jnp.broadcast_to(total, sum_ref.shape)
    load.wait()


def own_kernel(scale, q_ref, got_ref, cache_ref, cache_top_ref, cache_sum_ref, weight_hbm, out_ref, top_ref, sum_ref, weight_ref, sem):
    load = pltpu.make_async_copy(weight_hbm.at[EARLY : weight_hbm.shape[0] - LATE], weight_ref, sem)
    load.start()
    scores = prompt_scores(q_ref[...].astype(jnp.bfloat16), got_ref, 0, scale)
    top = jnp.max(functools.reduce(jnp.maximum, scores), axis=1, keepdims=True)
    top = jnp.maximum(top, cache_top_ref[...])
    exps = [jnp.exp(s - top) for s in scores]
    total = jnp.sum(functools.reduce(jnp.add, exps), axis=1, keepdims=True)
    near = jnp.exp(cache_top_ref[...] - top)
    out_ref[...] = prompt_sum(exps, got_ref, 0) + cache_ref[...] * near
    top_ref[...] = top
    sum_ref[...] = total + cache_sum_ref[...] * near
    load.wait()


def project_kernel(main_ref, top_ref, sum_ref, back_ref, weight0_ref, weight1_ref, out_ref, scratch):
    pieces, seqs, cols = out_ref.shape
    rows = main_ref.shape[0]
    heads = rows // seqs
    stats = jnp.concatenate([back_ref[rows:, :].astype(jnp.float32)] * (128 // 16), axis=0)
    stats = jnp.transpose(stats)
    far_top = stats[:, 0:1]
    far_sum = stats[:, 1:2] + stats[:, 2:3]
    top = jnp.maximum(top_ref[...], far_top)
    near = jnp.exp(top_ref[...] - top)
    far = jnp.exp(far_top - top)
    total = sum_ref[...] * near + far_sum * far
    scratch[...] = (main_ref[...] * near + back_ref[:rows, :].astype(jnp.float32) * far) / total
    attended = jnp.concatenate(
        [scratch[pl.ds(h, seqs, stride=heads), :].astype(jnp.bfloat16) for h in range(heads)], axis=1
    )
    parts = [0.0] * pieces
    at = 0
    for c in range(pieces):
        w = weight0_ref[:, c * cols : (c + 1) * cols]
        parts[c] += jnp.dot(attended[:, at : at + w.shape[0]], w, preferred_element_type=jnp.float32)
    at += weight0_ref.shape[0]
    for c in range(pieces):
        w = weight1_ref[:, c * cols : (c + 1) * cols]
        parts[c] += jnp.dot(attended[:, at : at + w.shape[0]], w, preferred_element_type=jnp.float32)
    at += weight1_ref.shape[0]
    for c in range(pieces):
        out_ref[c] = parts[c].astype(out_ref.dtype)


def vmem(n):
    return [pl.BlockSpec(memory_space=VMEM)] * n


def smem(n):
    return [pl.BlockSpec(memory_space=SMEM)] * n


def shards(
    queries,
    cache_keys,
    cache_values,
    context_lens,
    prompt_keys,
    prompt_values,
    prompt_lens,
    matching,
    dest_seq,
    out_weight,
):
    seqs, q_width = queries.shape
    ctx = cache_keys.shape[1]
    prompts, plen, _ = prompt_keys.shape
    pool = lax.axis_size("pool")
    pieces = lax.axis_size("tensor")
    out_cols = out_weight.shape[1]
    half = pool // 2
    rows = q_width // HD * seqs
    width = CAP * plen
    scale = 1.0 / math.sqrt(HD)
    swap = [(i, (i + half) % pool) for i in range(pool)]
    halves = [list(range(half)), list(range(half, pool))]
    in_hbm = lambda x: pltpu.with_memory_space_constraint(x, pltpu.HBM)
    anywhere = pl.BlockSpec(memory_space=pltpu.HBM)
    small = VMEM((rows, HD), jnp.float32)
    far_queries = lax.ppermute(queries, "pool", swap)
    packed = pl.pallas_call(
        functools.partial(pack_kernel, half),
        out_shape=jax.ShapeDtypeStruct((half, 4 * width + 16, HD), jnp.bfloat16),
        in_specs=[anywhere] * 5,
        out_specs=pl.BlockSpec(memory_space=VMEM),
        scratch_shapes=[SMEM((prompts,), jnp.int32)] * 3
        + [VMEM((prompts, plen, HD), jnp.bfloat16)] * 2
        + [pltpu.SemaphoreType.DMA((5,)), SMEM((pool,), jnp.int32)]
        + [SMEM((half * 2 * CAP,), jnp.int32)] * 2,
        compiler_params=pltpu.CompilerParams(vmem_limit_bytes=16 << 20),
        name="pack",
    )(*[in_hbm(x) for x in (matching.reshape(-1), dest_seq, prompt_lens, prompt_keys, prompt_values)])
    got = lax.all_to_all(packed, "pool", 0, 0, axis_index_groups=halves)
    cache, cache_top, cache_sum, heads_first, weight0 = pl.pallas_call(
        functools.partial(cache_kernel, scale),
        out_shape=[jax.ShapeDtypeStruct((rows, HD), jnp.float32)] * 4 + [VMEM((EARLY, out_cols), out_weight.dtype)],
        in_specs=smem(1) + vmem(3) + [anywhere],
        out_specs=vmem(5),
        scratch_shapes=[small, pltpu.SemaphoreType.DMA],
        compiler_params=pltpu.CompilerParams(vmem_limit_bytes=24 << 20),
        cost_estimate=pl.CostEstimate(flops=200_000_000, bytes_accessed=12_000_000, transcendentals=200_000),
        name="cache",
    )(*[in_hbm(x) for x in (context_lens, queries, cache_keys, cache_values, out_weight)])
    far_queries, cache = lax.optimization_barrier((far_queries, cache))
    back = pl.pallas_call(
        functools.partial(partner_kernel, scale),
        out_shape=jax.ShapeDtypeStruct((rows + 16, HD), jnp.bfloat16),
        in_specs=vmem(2),
        out_specs=pl.BlockSpec(memory_space=VMEM),
        scratch_shapes=[small],
        compiler_params=pltpu.CompilerParams(vmem_limit_bytes=16 << 20),
        name="partner",
    )(far_queries, got)
    back = lax.ppermute(back, "pool", swap)
    main, top, total, weight = pl.pallas_call(
        functools.partial(own_kernel, scale),
        out_shape=[jax.ShapeDtypeStruct((rows, HD), jnp.float32)] * 3 + [VMEM((out_weight.shape[0] - EARLY - LATE, out_cols), out_weight.dtype)],
        in_specs=vmem(5) + [anywhere],
        out_specs=vmem(4),
        scratch_shapes=[pltpu.SemaphoreType.DMA],
        compiler_params=pltpu.CompilerParams(vmem_limit_bytes=16 << 20),
        cost_estimate=pl.CostEstimate(flops=100_000_000, bytes_accessed=2_000_000, transcendentals=200_000),
        name="own",
    )(heads_first, got, cache, cache_top, cache_sum, in_hbm(out_weight))
    parts = pl.pallas_call(
        project_kernel,
        out_shape=jax.ShapeDtypeStruct((pieces, seqs, out_cols // pieces), jnp.bfloat16),
        in_specs=vmem(6),
        out_specs=pl.BlockSpec(memory_space=VMEM),
        scratch_shapes=[small],
        compiler_params=pltpu.CompilerParams(vmem_limit_bytes=24 << 20),
        name="project",
    )(main, top, total, back, weight0, weight)
    parts = lax.all_to_all(parts, "tensor", 0, 0)
    return jnp.sum(parts.astype(jnp.float32), axis=0).astype(jnp.bfloat16)


def solution(mesh):
    placed = (
        P("pool", "tensor"),
        P("pool", None, "tensor"),
        P("pool", None, "tensor"),
        P("pool"),
        P("pool", None, "tensor"),
        P("pool", None, "tensor"),
        P("pool"),
        P("pool", None),
        P("pool"),
        P("tensor", None),
    )
    return jax.shard_map(
        shards, mesh=mesh, in_specs=placed, out_specs=P("pool", "tensor"), check_vma=False
    )
```

```python
import functools
import math

import jax
import jax.numpy as jnp
from jax import lax
from jax.experimental import pallas as pl
from jax.experimental.pallas import tpu as pltpu
from jax.sharding import PartitionSpec as P

HD = 128
CAP = 2
EARLY = 256
LATE = 0
NEG = -(2.0**99)
VMEM = pltpu.VMEM
SMEM = pltpu.SMEM
NT = (((1,), (1,)), ((), ()))


def pack_kernel(
    half, owner_hbm, dest_hbm, len_hbm, keys_hbm, values_hbm, out_ref, owner_ref, dest_ref, len_ref, keys, values, sems, count, length, target
):
    prompts, plen, _ = keys.shape
    blocks = out_ref.shape[0]
    width = CAP * plen
    pairs = ((owner_hbm, owner_ref), (dest_hbm, dest_ref), (len_hbm, len_ref), (keys_hbm, keys), (values_hbm, values))
    loads = [pltpu.make_async_copy(a, b, sems.at[i]) for i, (a, b) in enumerate(pairs)]
    for load in loads:
        load.start()
    zeros = jnp.zeros((width, HD), jnp.bfloat16)
    for b in range(blocks):
        out_ref[b, width : 2 * width, :] = zeros
        out_ref[b, 3 * width : 4 * width, :] = zeros
    bits = half.bit_length() - 1
    my_half = lax.axis_index("pool") >> bits
    for i in range(2 * half):
        count[i] = 0
    for i in range(blocks * 2 * CAP):
        length[i] = 0
        target[i] = 0
    for load in loads[:3]:
        load.wait()
    places = []
    for p in range(prompts):
        group = owner_ref[p]
        rank = jnp.minimum(count[group], CAP - 1)
        count[group] = rank + 1
        block = group & (half - 1)
        other = (group >> bits) ^ my_half
        slot = block * (2 * CAP) + other * CAP + rank
        length[slot] = len_ref[p]
        target[slot] = dest_ref[p]
        places.append((block, other * 2 * width + rank * plen))
    row = lax.broadcasted_iota(jnp.int32, (16, 128), 0)
    lane = lax.broadcasted_iota(jnp.int32, (16, 128), 1)
    pos = lane % plen
    second = (lane // plen) % CAP == 1
    lower = row < 8
    for b in range(blocks):
        s = b * 2 * CAP
        limit = jnp.where(
            lower,
            jnp.where(second, length[s + 1], length[s]),
            jnp.where(second, length[s + 3], length[s + 2]),
        )
        code = jnp.where(
            lower,
            jnp.where(second, target[s + 1], target[s]),
            jnp.where(second, target[s + 3], target[s + 2]),
        )
        code = jnp.where(pos < limit, code, -1)
        out_ref[b, 4 * width :, :] = code.astype(jnp.float32).astype(jnp.bfloat16)
    for load in loads[3:]:
        load.wait()
    for p, (block, at) in enumerate(places):
        out_ref[block, pl.ds(pl.multiple_of(at, plen), plen), :] = keys[p]
        out_ref[block, pl.ds(pl.multiple_of(at + width, plen), plen), :] = values[p]


def split_heads(q_ref, scratch):
    seqs = q_ref.shape[0]
    heads = q_ref.shape[1] // HD
    for h in range(heads):
        scratch[h * seqs : (h + 1) * seqs, :] = q_ref[:, h * HD : (h + 1) * HD].astype(jnp.float32)
    return [scratch[pl.ds(s, heads, stride=seqs), :] for s in range(seqs)]


def prompt_scores(q, got_ref, other, scale):
    blocks, rows, _ = got_ref.shape
    width = (rows - 16) // 4
    at = other * 2 * width
    seq = lax.broadcasted_iota(jnp.int32, (q.shape[0], 128), 0) // 8
    left = lax.broadcasted_iota(jnp.int32, (8, 128), 1) < width
    out = []
    for b in range(0, blocks, 2):
        keys = jnp.concatenate([got_ref[b, at : at + width, :], got_ref[b + 1, at : at + width, :]], axis=0)
        s = lax.dot_general(q, keys, NT, preferred_element_type=jnp.float32) * scale
        meta0 = got_ref[b, 4 * width :, :].astype(jnp.float32)
        meta1 = got_ref[b + 1, 4 * width :, :].astype(jnp.float32)
        code = jnp.where(left, meta0[other * 8 : other * 8 + 8], meta1[other * 8 : other * 8 + 8])[0:1]
        out.append(jnp.where(seq == code.astype(jnp.int32), s, NEG))
    return out


def prompt_sum(weights, got_ref, other):
    blocks, rows, _ = got_ref.shape
    width = (rows - 16) // 4
    at = other * 2 * width + width
    total = None
    for i, b in enumerate(range(0, blocks, 2)):
        values = jnp.concatenate([got_ref[b, at : at + width, :], got_ref[b + 1, at : at + width, :]], axis=0)
        part = jnp.dot(weights[i].astype(jnp.bfloat16), values, preferred_element_type=jnp.float32)
        total = part if total is None else total + part
    return total


def partner_kernel(scale, q_ref, got_ref, out_ref, scratch):
    q = jnp.concatenate(split_heads(q_ref, scratch), axis=0).astype(jnp.bfloat16)
    scores = prompt_scores(q, got_ref, 1, scale)
    top = functools.reduce(jnp.maximum, scores)
    top = jnp.max(top, axis=1, keepdims=True).astype(jnp.bfloat16).astype(jnp.float32)
    exps = [jnp.exp(s - top) for s in scores]
    total = jnp.sum(functools.reduce(jnp.add, exps), axis=1, keepdims=True)
    rows = q.shape[0]
    out_ref[:rows, :] = prompt_sum(exps, got_ref, 1).astype(jnp.bfloat16)
    high = total.astype(jnp.bfloat16).astype(jnp.float32)
    lane = lax.broadcasted_iota(jnp.int32, (rows, 128), 1)
    stats = jnp.where(lane == 0, top, jnp.where(lane == 1, high, total - high))
    out_ref[rows:, :] = jnp.transpose(stats)[:16, :].astype(jnp.bfloat16)


def cache_kernel(scale, lens_ref, q_ref, keys_ref, values_ref, weight_hbm, out_ref, top_ref, sum_ref, q_out_ref, weight_ref, scratch, sem):
    load = pltpu.make_async_copy(weight_hbm.at[:EARLY], weight_ref, sem)
    load.start()
    seqs, ctx, _ = keys_ref.shape
    rows = split_heads(q_ref, scratch)
    q_out_ref[...] = jnp.concatenate(rows, axis=0)
    heads = rows[0].shape[0]
    col = lax.broadcasted_iota(jnp.int32, (heads, ctx), 1)
    scores = []
    for s in range(seqs):
        sc = lax.dot_general(rows[s].astype(jnp.bfloat16), keys_ref[s], NT, preferred_element_type=jnp.float32)
        scores.append(jnp.where(col < lens_ref[s], sc * scale, NEG))
    scores = jnp.concatenate(scores, axis=0)
    top = jnp.max(scores, axis=1, keepdims=True)
    exps = jnp.exp(scores - top)
    total = jnp.sum(exps, axis=1, keepdims=True)
    for s in range(seqs):
        w = exps[s * heads : (s + 1) * heads].astype(jnp.bfloat16)
        out_ref[s * heads : (s + 1) * heads, :] = jnp.dot(w, values_ref[s], preferred_element_type=jnp.float32)
    top_ref[...] = jnp.broadcast_to(top, top_ref.shape)
    sum_ref[...] = jnp.broadcast_to(total, sum_ref.shape)
    load.wait()


def own_kernel(scale, q_ref, got_ref, cache_ref, cache_top_ref, cache_sum_ref, weight_hbm, out_ref, top_ref, sum_ref, weight_ref, sem):
    load = pltpu.make_async_copy(weight_hbm.at[EARLY : weight_hbm.shape[0] - LATE], weight_ref, sem)
    load.start()
    scores = prompt_scores(q_ref[...].astype(jnp.bfloat16), got_ref, 0, scale)
    top = jnp.max(functools.reduce(jnp.maximum, scores), axis=1, keepdims=True)
    top = jnp.maximum(top, cache_top_ref[...])
    exps = [jnp.exp(s - top) for s in scores]
    total = jnp.sum(functools.reduce(jnp.add, exps), axis=1, keepdims=True)
    near = jnp.exp(cache_top_ref[...] - top)
    out_ref[...] = prompt_sum(exps, got_ref, 0) + cache_ref[...] * near
    top_ref[...] = top
    sum_ref[...] = total + cache_sum_ref[...] * near
    load.wait()


def project_kernel(main_ref, top_ref, sum_ref, back_ref, weight0_ref, weight1_ref, out_ref, scratch):
    pieces, seqs, cols = out_ref.shape
    rows = main_ref.shape[0]
    heads = rows // seqs
    stats = jnp.concatenate([back_ref[rows:, :].astype(jnp.float32)] * (128 // 16), axis=0)
    stats = jnp.transpose(stats)
    far_top = stats[:, 0:1]
    far_sum = stats[:, 1:2] + stats[:, 2:3]
    top = jnp.maximum(top_ref[...], far_top)
    near = jnp.exp(top_ref[...] - top)
    far = jnp.exp(far_top - top)
    total = sum_ref[...] * near + far_sum * far
    scratch[...] = (main_ref[...] * near + back_ref[:rows, :].astype(jnp.float32) * far) / total
    attended = jnp.concatenate(
        [scratch[pl.ds(h, seqs, stride=heads), :].astype(jnp.bfloat16) for h in range(heads)], axis=1
    )
    parts = [0.0] * pieces
    at = 0
    for c in range(pieces):
        w = weight0_ref[:, c * cols : (c + 1) * cols]
        parts[c] += jnp.dot(attended[:, at : at + w.shape[0]], w, preferred_element_type=jnp.float32)
    at += weight0_ref.shape[0]
    for c in range(pieces):
        w = weight1_ref[:, c * cols : (c + 1) * cols]
        parts[c] += jnp.dot(attended[:, at : at + w.shape[0]], w, preferred_element_type=jnp.float32)
    at += weight1_ref.shape[0]
    for c in range(pieces):
        out_ref[c] = parts[c].astype(out_ref.dtype)


def vmem(n):
    return [pl.BlockSpec(memory_space=VMEM)] * n


def smem(n):
    return [pl.BlockSpec(memory_space=SMEM)] * n


def shards(
    queries,
    cache_keys,
    cache_values,
    context_lens,
    prompt_keys,
    prompt_values,
    prompt_lens,
    matching,
    dest_seq,
    out_weight,
):
    seqs, q_width = queries.shape
    ctx = cache_keys.shape[1]
    prompts, plen, _ = prompt_keys.shape
    pool = lax.axis_size("pool")
    pieces = lax.axis_size("tensor")
    out_cols = out_weight.shape[1]
    half = pool // 2
    rows = q_width // HD * seqs
    width = CAP * plen
    scale = 1.0 / math.sqrt(HD)
    swap = [(i, (i + half) % pool) for i in range(pool)]
    halves = [list(range(half)), list(range(half, pool))]
    in_hbm = lambda x: pltpu.with_memory_space_constraint(x, pltpu.HBM)
    anywhere = pl.BlockSpec(memory_space=pltpu.HBM)
    small = VMEM((rows, HD), jnp.float32)
    far_queries = lax.ppermute(queries, "pool", swap)
    packed = pl.pallas_call(
        functools.partial(pack_kernel, half),
        out_shape=jax.ShapeDtypeStruct((half, 4 * width + 16, HD), jnp.bfloat16),
        in_specs=[anywhere] * 5,
        out_specs=pl.BlockSpec(memory_space=VMEM),
        scratch_shapes=[SMEM((prompts,), jnp.int32)] * 3
        + [VMEM((prompts, plen, HD), jnp.bfloat16)] * 2
        + [pltpu.SemaphoreType.DMA((5,)), SMEM((pool,), jnp.int32)]
        + [SMEM((half * 2 * CAP,), jnp.int32)] * 2,
        compiler_params=pltpu.CompilerParams(vmem_limit_bytes=16 << 20),
        name="pack",
    )(*[in_hbm(x) for x in (matching.reshape(-1), dest_seq, prompt_lens, prompt_keys, prompt_values)])
    got = lax.all_to_all(packed, "pool", 0, 0, axis_index_groups=halves)
    cache, cache_top, cache_sum, heads_first, weight0 = pl.pallas_call(
        functools.partial(cache_kernel, scale),
        out_shape=[jax.ShapeDtypeStruct((rows, HD), jnp.float32)] * 4 + [VMEM((EARLY, out_cols), out_weight.dtype)],
        in_specs=smem(1) + vmem(3) + [anywhere],
        out_specs=vmem(5),
        scratch_shapes=[small, pltpu.SemaphoreType.DMA],
        compiler_params=pltpu.CompilerParams(vmem_limit_bytes=24 << 20),
        cost_estimate=pl.CostEstimate(flops=200_000_000, bytes_accessed=12_000_000, transcendentals=200_000),
        name="cache",
    )(*[in_hbm(x) for x in (context_lens, queries, cache_keys, cache_values, out_weight)])
    far_queries, cache = lax.optimization_barrier((far_queries, cache))
    back = pl.pallas_call(
        functools.partial(partner_kernel, scale),
        out_shape=jax.ShapeDtypeStruct((rows + 16, HD), jnp.bfloat16),
        in_specs=vmem(2),
        out_specs=pl.BlockSpec(memory_space=VMEM),
        scratch_shapes=[small],
        compiler_params=pltpu.CompilerParams(vmem_limit_bytes=16 << 20),
        name="partner",
    )(far_queries, got)
    back = lax.ppermute(back, "pool", swap)
    main, top, total, weight = pl.pallas_call(
        functools.partial(own_kernel, scale),
        out_shape=[jax.ShapeDtypeStruct((rows, HD), jnp.float32)] * 3 + [VMEM((out_weight.shape[0] - EARLY - LATE, out_cols), out_weight.dtype)],
        in_specs=vmem(5) + [anywhere],
        out_specs=vmem(4),
        scratch_shapes=[pltpu.SemaphoreType.DMA],
        compiler_params=pltpu.CompilerParams(vmem_limit_bytes=16 << 20),
        cost_estimate=pl.CostEstimate(flops=100_000_000, bytes_accessed=2_000_000, transcendentals=200_000),
        name="own",
    )(heads_first, got, cache, cache_top, cache_sum, in_hbm(out_weight))
    parts = pl.pallas_call(
        project_kernel,
        out_shape=jax.ShapeDtypeStruct((pieces, seqs, out_cols // pieces), jnp.bfloat16),
        in_specs=vmem(6),
        out_specs=pl.BlockSpec(memory_space=VMEM),
        scratch_shapes=[small],
        compiler_params=pltpu.CompilerParams(vmem_limit_bytes=24 << 20),
        name="project",
    )(main, top, total, back, weight0, weight)
    second = lax.axis_index("tensor") % 2 == 1
    ring = [[i for i in range(pieces) if i % 2 == k] for k in range(2)]
    parts, second = lax.optimization_barrier((parts, second))
    parts = parts.reshape(pieces // 2, 2, seqs, out_cols // pieces)
    parts = lax.all_to_all(parts, "tensor", 0, 0, axis_index_groups=ring)
    parts = jnp.sum(parts.astype(jnp.float32), axis=0)
    away = jnp.where(second, parts[0], parts[1]).astype(jnp.bfloat16)
    near = jnp.where(second, parts[1], parts[0])
    away = lax.ppermute(away, "tensor", [(i, i ^ 1) for i in range(pieces)])
    return (near + away.astype(jnp.float32)).astype(jnp.bfloat16)


def solution(mesh):
    placed = (
        P("pool", "tensor"),
        P("pool", None, "tensor"),
        P("pool", None, "tensor"),
        P("pool"),
        P("pool", None, "tensor"),
        P("pool", None, "tensor"),
        P("pool"),
        P("pool", None),
        P("pool"),
        P("tensor", None),
    )
    return jax.shard_map(
        shards, mesh=mesh, in_specs=placed, out_specs=P("pool", "tensor"), check_vma=False
    )
```

```python
import functools
import math

import jax
import jax.numpy as jnp
from jax import lax
from jax.experimental import pallas as pl
from jax.experimental.pallas import tpu as pltpu
from jax.sharding import PartitionSpec as P

HD = 128
CAP = 2
EARLY = 256
LATE = 0
NEG = -(2.0**99)
VMEM = pltpu.VMEM
SMEM = pltpu.SMEM
NT = (((1,), (1,)), ((), ()))


def pack_kernel(
    half, owner_hbm, dest_hbm, len_hbm, keys_hbm, values_hbm, out_ref, owner_ref, dest_ref, len_ref, keys, values, sems, count, length, target
):
    prompts, plen, _ = keys.shape
    blocks = out_ref.shape[0]
    width = CAP * plen
    pairs = ((owner_hbm, owner_ref), (dest_hbm, dest_ref), (len_hbm, len_ref), (keys_hbm, keys), (values_hbm, values))
    loads = [pltpu.make_async_copy(a, b, sems.at[i]) for i, (a, b) in enumerate(pairs)]
    for load in loads:
        load.start()
    zeros = jnp.zeros((width, HD), jnp.bfloat16)
    for b in range(blocks):
        out_ref[b, width : 2 * width, :] = zeros
        out_ref[b, 3 * width : 4 * width, :] = zeros
    bits = half.bit_length() - 1
    my_half = lax.axis_index("pool") >> bits
    for i in range(2 * half):
        count[i] = 0
    for i in range(blocks * 2 * CAP):
        length[i] = 0
        target[i] = 0
    for load in loads[:3]:
        load.wait()
    places = []
    for p in range(prompts):
        group = owner_ref[p]
        rank = jnp.minimum(count[group], CAP - 1)
        count[group] = rank + 1
        block = group & (half - 1)
        other = (group >> bits) ^ my_half
        slot = block * (2 * CAP) + other * CAP + rank
        length[slot] = len_ref[p]
        target[slot] = dest_ref[p]
        places.append((block, other * 2 * width + rank * plen))
    row = lax.broadcasted_iota(jnp.int32, (8, 128), 0)
    lane = lax.broadcasted_iota(jnp.int32, (8, 128), 1)
    pos = lane % plen
    second = (lane // plen) % CAP == 1
    lower = row < 4
    for b in range(blocks):
        s = b * 2 * CAP
        limit = jnp.where(
            lower,
            jnp.where(second, length[s + 1], length[s]),
            jnp.where(second, length[s + 3], length[s + 2]),
        )
        code = jnp.where(
            lower,
            jnp.where(second, target[s + 1], target[s]),
            jnp.where(second, target[s + 3], target[s + 2]),
        )
        code = jnp.where(pos < limit, code, -1)
        out_ref[b, 4 * width :, :] = code.astype(jnp.float32).astype(jnp.bfloat16)
    for load in loads[3:]:
        load.wait()
    for p, (block, at) in enumerate(places):
        out_ref[block, pl.ds(pl.multiple_of(at, plen), plen), :] = keys[p]
        out_ref[block, pl.ds(pl.multiple_of(at + width, plen), plen), :] = values[p]


def split_heads(q_ref, scratch):
    seqs = q_ref.shape[0]
    heads = q_ref.shape[1] // HD
    for h in range(heads):
        scratch[h * seqs : (h + 1) * seqs, :] = q_ref[:, h * HD : (h + 1) * HD].astype(jnp.float32)
    return [scratch[pl.ds(s, heads, stride=seqs), :] for s in range(seqs)]


def prompt_scores(q, got_ref, other, scale):
    blocks, rows, _ = got_ref.shape
    width = (rows - 8) // 4
    at = other * 2 * width
    seq = lax.broadcasted_iota(jnp.int32, (q.shape[0], 128), 0) // 8
    left = lax.broadcasted_iota(jnp.int32, (1, 128), 1) < width
    out = []
    for b in range(0, blocks, 2):
        keys = jnp.concatenate([got_ref[b, at : at + width, :], got_ref[b + 1, at : at + width, :]], axis=0)
        s = lax.dot_general(q, keys, NT, preferred_element_type=jnp.float32) * scale
        meta0 = got_ref[b, 4 * width :, :].astype(jnp.float32)
        meta1 = got_ref[b + 1, 4 * width :, :].astype(jnp.float32)
        code = jnp.where(left, meta0[other * 4 : other * 4 + 1], meta1[other * 4 : other * 4 + 1])
        out.append(jnp.where(seq == code.astype(jnp.int32), s, NEG))
    return out


def prompt_sum(weights, got_ref, other):
    blocks, rows, _ = got_ref.shape
    width = (rows - 8) // 4
    at = other * 2 * width + width
    total = None
    for i, b in enumerate(range(0, blocks, 2)):
        values = jnp.concatenate([got_ref[b, at : at + width, :], got_ref[b + 1, at : at + width, :]], axis=0)
        part = jnp.dot(weights[i].astype(jnp.bfloat16), values, preferred_element_type=jnp.float32)
        total = part if total is None else total + part
    return total


def partner_kernel(scale, q_ref, got_ref, out_ref, scratch):
    q = jnp.concatenate(split_heads(q_ref, scratch), axis=0).astype(jnp.bfloat16)
    scores = prompt_scores(q, got_ref, 1, scale)
    top = functools.reduce(jnp.maximum, scores)
    top = jnp.max(top, axis=1, keepdims=True).astype(jnp.bfloat16).astype(jnp.float32)
    exps = [jnp.exp(s - top) for s in scores]
    total = jnp.sum(functools.reduce(jnp.add, exps), axis=1, keepdims=True)
    rows = q.shape[0]
    out_ref[:rows, :] = prompt_sum(exps, got_ref, 1).astype(jnp.bfloat16)
    high = total.astype(jnp.bfloat16).astype(jnp.float32)
    lane = lax.broadcasted_iota(jnp.int32, (rows, 128), 1)
    stats = jnp.where(lane == 0, top, jnp.where(lane == 1, high, total - high))
    out_ref[rows:, :] = jnp.transpose(stats)[:16, :].astype(jnp.bfloat16)


def cache_kernel(scale, lens_ref, q_ref, keys_ref, values_ref, weight_hbm, out_ref, top_ref, sum_ref, q_out_ref, weight_ref, scratch, sem):
    load = pltpu.make_async_copy(weight_hbm.at[:EARLY], weight_ref, sem)
    load.start()
    seqs, ctx, _ = keys_ref.shape
    rows = split_heads(q_ref, scratch)
    q_out_ref[...] = jnp.concatenate(rows, axis=0)
    heads = rows[0].shape[0]
    col = lax.broadcasted_iota(jnp.int32, (heads, ctx), 1)
    scores = []
    for s in range(seqs):
        sc = lax.dot_general(rows[s].astype(jnp.bfloat16), keys_ref[s], NT, preferred_element_type=jnp.float32)
        scores.append(jnp.where(col < lens_ref[s], sc * scale, NEG))
    scores = jnp.concatenate(scores, axis=0)
    top = jnp.max(scores, axis=1, keepdims=True)
    exps = jnp.exp(scores - top)
    total = jnp.sum(exps, axis=1, keepdims=True)
    for s in range(seqs):
        w = exps[s * heads : (s + 1) * heads].astype(jnp.bfloat16)
        out_ref[s * heads : (s + 1) * heads, :] = jnp.dot(w, values_ref[s], preferred_element_type=jnp.float32)
    top_ref[...] = jnp.broadcast_to(top, top_ref.shape)
    sum_ref[...] = jnp.broadcast_to(total, sum_ref.shape)
    load.wait()


def own_kernel(scale, q_ref, got_ref, cache_ref, cache_top_ref, cache_sum_ref, weight_hbm, out_ref, top_ref, sum_ref, weight_ref, sem):
    load = pltpu.make_async_copy(weight_hbm.at[EARLY : weight_hbm.shape[0] - LATE], weight_ref, sem)
    load.start()
    scores = prompt_scores(q_ref[...].astype(jnp.bfloat16), got_ref, 0, scale)
    top = jnp.max(functools.reduce(jnp.maximum, scores), axis=1, keepdims=True)
    top = jnp.maximum(top, cache_top_ref[...])
    exps = [jnp.exp(s - top) for s in scores]
    total = jnp.sum(functools.reduce(jnp.add, exps), axis=1, keepdims=True)
    near = jnp.exp(cache_top_ref[...] - top)
    out_ref[...] = prompt_sum(exps, got_ref, 0) + cache_ref[...] * near
    top_ref[...] = top
    sum_ref[...] = total + cache_sum_ref[...] * near
    load.wait()


def project_kernel(main_ref, top_ref, sum_ref, back_ref, weight0_ref, weight1_ref, out_ref, scratch):
    pieces, seqs, cols = out_ref.shape
    rows = main_ref.shape[0]
    heads = rows // seqs
    stats = jnp.concatenate([back_ref[rows:, :].astype(jnp.float32)] * (128 // 16), axis=0)
    stats = jnp.transpose(stats)
    far_top = stats[:, 0:1]
    far_sum = stats[:, 1:2] + stats[:, 2:3]
    top = jnp.maximum(top_ref[...], far_top)
    near = jnp.exp(top_ref[...] - top)
    far = jnp.exp(far_top - top)
    total = sum_ref[...] * near + far_sum * far
    scratch[...] = (main_ref[...] * near + back_ref[:rows, :].astype(jnp.float32) * far) / total
    attended = jnp.concatenate(
        [scratch[pl.ds(h, seqs, stride=heads), :].astype(jnp.bfloat16) for h in range(heads)], axis=1
    )
    parts = [0.0] * pieces
    at = 0
    for c in range(pieces):
        w = weight0_ref[:, c * cols : (c + 1) * cols]
        parts[c] += jnp.dot(attended[:, at : at + w.shape[0]], w, preferred_element_type=jnp.float32)
    at += weight0_ref.shape[0]
    for c in range(pieces):
        w = weight1_ref[:, c * cols : (c + 1) * cols]
        parts[c] += jnp.dot(attended[:, at : at + w.shape[0]], w, preferred_element_type=jnp.float32)
    at += weight1_ref.shape[0]
    for c in range(pieces):
        out_ref[c] = parts[c].astype(out_ref.dtype)


def vmem(n):
    return [pl.BlockSpec(memory_space=VMEM)] * n


def smem(n):
    return [pl.BlockSpec(memory_space=SMEM)] * n


def shards(
    queries,
    cache_keys,
    cache_values,
    context_lens,
    prompt_keys,
    prompt_values,
    prompt_lens,
    matching,
    dest_seq,
    out_weight,
):
    seqs, q_width = queries.shape
    ctx = cache_keys.shape[1]
    prompts, plen, _ = prompt_keys.shape
    pool = lax.axis_size("pool")
    pieces = lax.axis_size("tensor")
    out_cols = out_weight.shape[1]
    half = pool // 2
    rows = q_width // HD * seqs
    width = CAP * plen
    scale = 1.0 / math.sqrt(HD)
    swap = [(i, (i + half) % pool) for i in range(pool)]
    halves = [list(range(half)), list(range(half, pool))]
    in_hbm = lambda x: pltpu.with_memory_space_constraint(x, pltpu.HBM)
    anywhere = pl.BlockSpec(memory_space=pltpu.HBM)
    small = VMEM((rows, HD), jnp.float32)
    far_queries = lax.ppermute(queries, "pool", swap)
    packed = pl.pallas_call(
        functools.partial(pack_kernel, half),
        out_shape=jax.ShapeDtypeStruct((half, 4 * width + 8, HD), jnp.bfloat16),
        in_specs=[anywhere] * 5,
        out_specs=pl.BlockSpec(memory_space=VMEM),
        scratch_shapes=[SMEM((prompts,), jnp.int32)] * 3
        + [VMEM((prompts, plen, HD), jnp.bfloat16)] * 2
        + [pltpu.SemaphoreType.DMA((5,)), SMEM((pool,), jnp.int32)]
        + [SMEM((half * 2 * CAP,), jnp.int32)] * 2,
        compiler_params=pltpu.CompilerParams(vmem_limit_bytes=16 << 20),
        name="pack",
    )(*[in_hbm(x) for x in (matching.reshape(-1), dest_seq, prompt_lens, prompt_keys, prompt_values)])
    got = lax.all_to_all(packed, "pool", 0, 0, axis_index_groups=halves)
    cache, cache_top, cache_sum, heads_first, weight0 = pl.pallas_call(
        functools.partial(cache_kernel, scale),
        out_shape=[jax.ShapeDtypeStruct((rows, HD), jnp.float32)] * 4 + [VMEM((EARLY, out_cols), out_weight.dtype)],
        in_specs=smem(1) + vmem(3) + [anywhere],
        out_specs=vmem(5),
        scratch_shapes=[small, pltpu.SemaphoreType.DMA],
        compiler_params=pltpu.CompilerParams(vmem_limit_bytes=24 << 20),
        cost_estimate=pl.CostEstimate(flops=200_000_000, bytes_accessed=12_000_000, transcendentals=200_000),
        name="cache",
    )(*[in_hbm(x) for x in (context_lens, queries, cache_keys, cache_values, out_weight)])
    far_queries, cache = lax.optimization_barrier((far_queries, cache))
    back = pl.pallas_call(
        functools.partial(partner_kernel, scale),
        out_shape=jax.ShapeDtypeStruct((rows + 16, HD), jnp.bfloat16),
        in_specs=vmem(2),
        out_specs=pl.BlockSpec(memory_space=VMEM),
        scratch_shapes=[small],
        compiler_params=pltpu.CompilerParams(vmem_limit_bytes=16 << 20),
        name="partner",
    )(far_queries, got)
    back = lax.ppermute(back, "pool", swap)
    main, top, total, weight = pl.pallas_call(
        functools.partial(own_kernel, scale),
        out_shape=[jax.ShapeDtypeStruct((rows, HD), jnp.float32)] * 3 + [VMEM((out_weight.shape[0] - EARLY - LATE, out_cols), out_weight.dtype)],
        in_specs=vmem(5) + [anywhere],
        out_specs=vmem(4),
        scratch_shapes=[pltpu.SemaphoreType.DMA],
        compiler_params=pltpu.CompilerParams(vmem_limit_bytes=16 << 20),
        cost_estimate=pl.CostEstimate(flops=100_000_000, bytes_accessed=2_000_000, transcendentals=200_000),
        name="own",
    )(heads_first, got, cache, cache_top, cache_sum, in_hbm(out_weight))
    parts = pl.pallas_call(
        project_kernel,
        out_shape=jax.ShapeDtypeStruct((pieces, seqs, out_cols // pieces), jnp.bfloat16),
        in_specs=vmem(6),
        out_specs=pl.BlockSpec(memory_space=VMEM),
        scratch_shapes=[small],
        compiler_params=pltpu.CompilerParams(vmem_limit_bytes=24 << 20),
        name="project",
    )(main, top, total, back, weight0, weight)
    second = lax.axis_index("tensor") % 2 == 1
    ring = [[i for i in range(pieces) if i % 2 == k] for k in range(2)]
    parts, second = lax.optimization_barrier((parts, second))
    parts = parts.reshape(pieces // 2, 2, seqs, out_cols // pieces)
    parts = lax.all_to_all(parts, "tensor", 0, 0, axis_index_groups=ring)
    parts = jnp.sum(parts.astype(jnp.float32), axis=0)
    away = jnp.where(second, parts[0], parts[1]).astype(jnp.bfloat16)
    near = jnp.where(second, parts[1], parts[0])
    away = lax.ppermute(away, "tensor", [(i, i ^ 1) for i in range(pieces)])
    return (near + away.astype(jnp.float32)).astype(jnp.bfloat16)


def solution(mesh):
    placed = (
        P("pool", "tensor"),
        P("pool", None, "tensor"),
        P("pool", None, "tensor"),
        P("pool"),
        P("pool", None, "tensor"),
        P("pool", None, "tensor"),
        P("pool"),
        P("pool", None),
        P("pool"),
        P("tensor", None),
    )
    return jax.shard_map(
        shards, mesh=mesh, in_specs=placed, out_specs=P("pool", "tensor"), check_vma=False
    )
```

```python
import functools
import math

import jax
import jax.numpy as jnp
from jax import lax
from jax.experimental import pallas as pl
from jax.experimental.pallas import tpu as pltpu
from jax.sharding import PartitionSpec as P

HD = 128
CAP = 2
GROUP = 4
EARLY = 256
LATE = 128
NEG = -(2.0**99)
VMEM = pltpu.VMEM
SMEM = pltpu.SMEM
NT = (((1,), (1,)), ((), ()))


def pack_kernel(
    half, owner_hbm, dest_hbm, len_hbm, keys_hbm, values_hbm, out_ref, owner_ref, dest_ref, len_ref, keys, values, sems, count, length, target
):
    prompts, plen, _ = keys.shape
    blocks = out_ref.shape[0]
    width = CAP * plen
    pairs = ((owner_hbm, owner_ref), (dest_hbm, dest_ref), (len_hbm, len_ref), (keys_hbm, keys), (values_hbm, values))
    loads = [pltpu.make_async_copy(a, b, sems.at[i]) for i, (a, b) in enumerate(pairs)]
    for load in loads:
        load.start()
    zeros = jnp.zeros((width, HD), jnp.bfloat16)
    for b in range(blocks):
        out_ref[b, width : 2 * width, :] = zeros
        out_ref[b, 3 * width : 4 * width, :] = zeros
    bits = half.bit_length() - 1
    my_half = lax.axis_index("pool") >> bits
    for i in range(2 * half):
        count[i] = 0
    for i in range(blocks * 2 * CAP):
        length[i] = 0
        target[i] = 0
    for load in loads[:3]:
        load.wait()
    places = []
    for p in range(prompts):
        group = owner_ref[p]
        rank = jnp.minimum(count[group], CAP - 1)
        count[group] = rank + 1
        block = group & (half - 1)
        other = (group >> bits) ^ my_half
        slot = block * (2 * CAP) + other * CAP + rank
        length[slot] = len_ref[p]
        target[slot] = dest_ref[p]
        places.append((block, other * 2 * width + rank * plen))
    row = lax.broadcasted_iota(jnp.int32, (16, 128), 0)
    lane = lax.broadcasted_iota(jnp.int32, (16, 128), 1)
    pos = lane % plen
    second = (lane // plen) % CAP == 1
    lower = row < 8
    for b in range(blocks):
        s = b * 2 * CAP
        limit = jnp.where(
            lower,
            jnp.where(second, length[s + 1], length[s]),
            jnp.where(second, length[s + 3], length[s + 2]),
        )
        code = jnp.where(
            lower,
            jnp.where(second, target[s + 1], target[s]),
            jnp.where(second, target[s + 3], target[s + 2]),
        )
        code = jnp.where(pos < limit, code, -1)
        out_ref[b, 4 * width :, :] = code.astype(jnp.float32).astype(jnp.bfloat16)
    for load in loads[3:]:
        load.wait()
    for p, (block, at) in enumerate(places):
        out_ref[block, pl.ds(pl.multiple_of(at, plen), plen), :] = keys[p]
        out_ref[block, pl.ds(pl.multiple_of(at + width, plen), plen), :] = values[p]


def split_heads(q_ref, scratch):
    seqs = q_ref.shape[0]
    heads = q_ref.shape[1] // HD
    for h in range(heads):
        scratch[h * seqs : (h + 1) * seqs, :] = q_ref[:, h * HD : (h + 1) * HD].astype(jnp.float32)
    return [scratch[pl.ds(s, heads, stride=seqs), :] for s in range(seqs)]


def group(ref, b, at, width):
    return jnp.concatenate([ref[b + i, at : at + width, :] for i in range(GROUP)], axis=0)


def prompt_scores(q, got_ref, other, scale):
    blocks, rows, _ = got_ref.shape
    width = (rows - 16) // 4
    seq = lax.broadcasted_iota(jnp.int32, (q.shape[0], 128), 0) // 8
    left = lax.broadcasted_iota(jnp.int32, (1, 128), 1) < width
    out = []
    for b in range(0, blocks, GROUP):
        keys = group(got_ref, b, other * 2 * width, width)
        s = lax.dot_general(q, keys, NT, preferred_element_type=jnp.float32) * scale
        for i in range(0, GROUP, 2):
            meta = [got_ref[b + i + k, 4 * width :, :].astype(jnp.float32)[other * 8 : other * 8 + 1] for k in range(2)]
            code = jnp.where(left, meta[0], meta[1]).astype(jnp.int32)
            out.append(jnp.where(seq == code, s[:, i * width : (i + 2) * width], NEG))
    return out


def prompt_sum(weights, got_ref, other):
    blocks, rows, _ = got_ref.shape
    width = (rows - 16) // 4
    step = GROUP // 2
    total = None
    for i in range(0, len(weights), step):
        values = group(got_ref, 2 * i, other * 2 * width + width, width)
        part = jnp.concatenate([w.astype(jnp.bfloat16) for w in weights[i : i + step]], axis=1)
        part = jnp.dot(part, values, preferred_element_type=jnp.float32)
        total = part if total is None else total + part
    return total


def partner_kernel(scale, q_ref, got_ref, out_ref, scratch):
    q = jnp.concatenate(split_heads(q_ref, scratch), axis=0).astype(jnp.bfloat16)
    scores = prompt_scores(q, got_ref, 1, scale)
    top = functools.reduce(jnp.maximum, scores)
    top = jnp.max(top, axis=1, keepdims=True).astype(jnp.bfloat16).astype(jnp.float32)
    exps = [jnp.exp(s - top) for s in scores]
    total = jnp.sum(functools.reduce(jnp.add, exps), axis=1, keepdims=True)
    rows = q.shape[0]
    out_ref[:rows, :] = prompt_sum(exps, got_ref, 1).astype(jnp.bfloat16)
    high = total.astype(jnp.bfloat16).astype(jnp.float32)
    lane = lax.broadcasted_iota(jnp.int32, (rows, 128), 1)
    stats = jnp.where(lane == 0, top, jnp.where(lane == 1, high, total - high))
    out_ref[rows:, :] = jnp.transpose(stats)[:16, :].astype(jnp.bfloat16)


def cache_kernel(scale, lens_ref, q_ref, keys_ref, values_ref, weight_hbm, out_ref, top_ref, sum_ref, q_out_ref, weight_ref, scratch, sem):
    load = pltpu.make_async_copy(weight_hbm.at[:EARLY], weight_ref, sem)
    load.start()
    seqs, ctx, _ = keys_ref.shape
    rows = split_heads(q_ref, scratch)
    q_out_ref[...] = jnp.concatenate(rows, axis=0)
    heads = rows[0].shape[0]
    col = lax.broadcasted_iota(jnp.int32, (heads, ctx), 1)
    scores = []
    for s in range(seqs):
        sc = lax.dot_general(rows[s].astype(jnp.bfloat16), keys_ref[s], NT, preferred_element_type=jnp.float32)
        scores.append(jnp.where(col < lens_ref[s], sc * scale, NEG))
    scores = jnp.concatenate(scores, axis=0)
    top = jnp.max(scores, axis=1, keepdims=True)
    exps = jnp.exp(scores - top)
    total = jnp.sum(exps, axis=1, keepdims=True)
    for s in range(seqs):
        w = exps[s * heads : (s + 1) * heads].astype(jnp.bfloat16)
        out_ref[s * heads : (s + 1) * heads, :] = jnp.dot(w, values_ref[s], preferred_element_type=jnp.float32)
    top_ref[...] = jnp.broadcast_to(top, top_ref.shape)
    sum_ref[...] = jnp.broadcast_to(total, sum_ref.shape)
    load.wait()


def own_kernel(scale, q_ref, got_ref, cache_ref, cache_top_ref, cache_sum_ref, weight_hbm, out_ref, top_ref, sum_ref, weight_ref, sem):
    load = pltpu.make_async_copy(weight_hbm.at[EARLY : weight_hbm.shape[0] - LATE], weight_ref, sem)
    load.start()
    scores = prompt_scores(q_ref[...].astype(jnp.bfloat16), got_ref, 0, scale)
    top = jnp.max(functools.reduce(jnp.maximum, scores), axis=1, keepdims=True)
    top = jnp.maximum(top, cache_top_ref[...])
    exps = [jnp.exp(s - top) for s in scores]
    total = jnp.sum(functools.reduce(jnp.add, exps), axis=1, keepdims=True)
    near = jnp.exp(cache_top_ref[...] - top)
    out_ref[...] = prompt_sum(exps, got_ref, 0) + cache_ref[...] * near
    top_ref[...] = top
    sum_ref[...] = total + cache_sum_ref[...] * near
    load.wait()


def project_kernel(main_ref, top_ref, sum_ref, back_ref, weight0_ref, weight1_ref, weight_hbm, out_ref, scratch, weight2_ref, sem):
    load = pltpu.make_async_copy(weight_hbm.at[weight_hbm.shape[0] - LATE :], weight2_ref, sem)
    load.start()
    pieces, seqs, cols = out_ref.shape
    rows = main_ref.shape[0]
    heads = rows // seqs
    stats = jnp.concatenate([back_ref[rows:, :].astype(jnp.float32)] * (128 // 16), axis=0)
    stats = jnp.transpose(stats)
    far_top = stats[:, 0:1]
    far_sum = stats[:, 1:2] + stats[:, 2:3]
    top = jnp.maximum(top_ref[...], far_top)
    near = jnp.exp(top_ref[...] - top)
    far = jnp.exp(far_top - top)
    total = sum_ref[...] * near + far_sum * far
    scratch[...] = (main_ref[...] * near + back_ref[:rows, :].astype(jnp.float32) * far) / total
    attended = jnp.concatenate(
        [scratch[pl.ds(h, seqs, stride=heads), :].astype(jnp.bfloat16) for h in range(heads)], axis=1
    )
    parts = [0.0] * pieces
    at = 0
    for weight_ref in (weight0_ref, weight1_ref, weight2_ref):
        if weight_ref is weight2_ref:
            load.wait()
        depth = weight_ref.shape[0]
        for c in range(pieces):
            weight = weight_ref[:, c * cols : (c + 1) * cols]
            parts[c] += jnp.dot(attended[:, at : at + depth], weight, preferred_element_type=jnp.float32)
        at += depth
    for c in range(pieces):
        out_ref[c] = parts[c].astype(out_ref.dtype)


def vmem(n):
    return [pl.BlockSpec(memory_space=VMEM)] * n


def smem(n):
    return [pl.BlockSpec(memory_space=SMEM)] * n


def shards(
    queries,
    cache_keys,
    cache_values,
    context_lens,
    prompt_keys,
    prompt_values,
    prompt_lens,
    matching,
    dest_seq,
    out_weight,
):
    seqs, q_width = queries.shape
    ctx = cache_keys.shape[1]
    prompts, plen, _ = prompt_keys.shape
    pool = lax.axis_size("pool")
    pieces = lax.axis_size("tensor")
    out_cols = out_weight.shape[1]
    half = pool // 2
    rows = q_width // HD * seqs
    width = CAP * plen
    scale = 1.0 / math.sqrt(HD)
    swap = [(i, (i + half) % pool) for i in range(pool)]
    halves = [list(range(half)), list(range(half, pool))]
    in_hbm = lambda x: pltpu.with_memory_space_constraint(x, pltpu.HBM)
    anywhere = pl.BlockSpec(memory_space=pltpu.HBM)
    small = VMEM((rows, HD), jnp.float32)
    far_queries = lax.ppermute(queries, "pool", swap)
    packed = pl.pallas_call(
        functools.partial(pack_kernel, half),
        out_shape=jax.ShapeDtypeStruct((half, 4 * width + 16, HD), jnp.bfloat16),
        in_specs=[anywhere] * 5,
        out_specs=pl.BlockSpec(memory_space=VMEM),
        scratch_shapes=[SMEM((prompts,), jnp.int32)] * 3
        + [VMEM((prompts, plen, HD), jnp.bfloat16)] * 2
        + [pltpu.SemaphoreType.DMA((5,)), SMEM((pool,), jnp.int32)]
        + [SMEM((half * 2 * CAP,), jnp.int32)] * 2,
        compiler_params=pltpu.CompilerParams(vmem_limit_bytes=16 << 20),
        name="pack",
    )(*[in_hbm(x) for x in (matching.reshape(-1), dest_seq, prompt_lens, prompt_keys, prompt_values)])
    got = lax.all_to_all(packed, "pool", 0, 0, axis_index_groups=halves)
    cache, cache_top, cache_sum, heads_first, weight0 = pl.pallas_call(
        functools.partial(cache_kernel, scale),
        out_shape=[jax.ShapeDtypeStruct((rows, HD), jnp.float32)] * 4 + [VMEM((EARLY, out_cols), out_weight.dtype)],
        in_specs=smem(1) + vmem(3) + [anywhere],
        out_specs=vmem(5),
        scratch_shapes=[small, pltpu.SemaphoreType.DMA],
        compiler_params=pltpu.CompilerParams(vmem_limit_bytes=24 << 20),
        cost_estimate=pl.CostEstimate(flops=200_000_000, bytes_accessed=12_000_000, transcendentals=200_000),
        name="cache",
    )(*[in_hbm(x) for x in (context_lens, queries, cache_keys, cache_values, out_weight)])
    far_queries, cache = lax.optimization_barrier((far_queries, cache))
    back = pl.pallas_call(
        functools.partial(partner_kernel, scale),
        out_shape=jax.ShapeDtypeStruct((rows + 16, HD), jnp.bfloat16),
        in_specs=vmem(2),
        out_specs=pl.BlockSpec(memory_space=VMEM),
        scratch_shapes=[small],
        compiler_params=pltpu.CompilerParams(vmem_limit_bytes=16 << 20),
        name="partner",
    )(far_queries, got)
    back = lax.ppermute(back, "pool", swap)
    main, top, total, weight = pl.pallas_call(
        functools.partial(own_kernel, scale),
        out_shape=[jax.ShapeDtypeStruct((rows, HD), jnp.float32)] * 3 + [VMEM((out_weight.shape[0] - EARLY - LATE, out_cols), out_weight.dtype)],
        in_specs=vmem(5) + [anywhere],
        out_specs=vmem(4),
        scratch_shapes=[pltpu.SemaphoreType.DMA],
        compiler_params=pltpu.CompilerParams(vmem_limit_bytes=16 << 20),
        cost_estimate=pl.CostEstimate(flops=100_000_000, bytes_accessed=2_000_000, transcendentals=200_000),
        name="own",
    )(heads_first, got, cache, cache_top, cache_sum, in_hbm(out_weight))
    parts = pl.pallas_call(
        project_kernel,
        out_shape=jax.ShapeDtypeStruct((pieces, seqs, out_cols // pieces), jnp.bfloat16),
        in_specs=vmem(6) + [anywhere],
        out_specs=pl.BlockSpec(memory_space=VMEM),
        scratch_shapes=[small, VMEM((LATE, out_cols), out_weight.dtype), pltpu.SemaphoreType.DMA],
        compiler_params=pltpu.CompilerParams(vmem_limit_bytes=24 << 20),
        name="project",
    )(main, top, total, back, weight0, weight, in_hbm(out_weight))
    second = lax.axis_index("tensor") % 2 == 1
    ring = [[i for i in range(pieces) if i % 2 == k] for k in range(2)]
    parts, second = lax.optimization_barrier((parts, second))
    parts = parts.reshape(pieces // 2, 2, seqs, out_cols // pieces)
    parts = lax.all_to_all(parts, "tensor", 0, 0, axis_index_groups=ring)
    parts = jnp.sum(parts.astype(jnp.float32), axis=0)
    away = jnp.where(second, parts[0], parts[1]).astype(jnp.bfloat16)
    near = jnp.where(second, parts[1], parts[0])
    away = lax.ppermute(away, "tensor", [(i, i ^ 1) for i in range(pieces)])
    return (near + away.astype(jnp.float32)).astype(jnp.bfloat16)


def solution(mesh):
    placed = (
        P("pool", "tensor"),
        P("pool", None, "tensor"),
        P("pool", None, "tensor"),
        P("pool"),
        P("pool", None, "tensor"),
        P("pool", None, "tensor"),
        P("pool"),
        P("pool", None),
        P("pool"),
        P("tensor", None),
    )
    return jax.shard_map(
        shards, mesh=mesh, in_specs=placed, out_specs=P("pool", "tensor"), check_vma=False
    )
```

```python
import functools
import math

import jax
import jax.numpy as jnp
from jax import lax
from jax.experimental import pallas as pl
from jax.experimental.pallas import tpu as pltpu
from jax.sharding import PartitionSpec as P

HD = 128
CAP = 2
GROUP = 4
EARLY = 256
LATE = 512
NEG = -(2.0**99)
VMEM = pltpu.VMEM
SMEM = pltpu.SMEM
NT = (((1,), (1,)), ((), ()))


def pack_kernel(
    half, owner_hbm, dest_hbm, len_hbm, keys_hbm, values_hbm, out_ref, owner_ref, dest_ref, len_ref, keys, values, sems, count, length, target
):
    prompts, plen, _ = keys.shape
    blocks = out_ref.shape[0]
    width = CAP * plen
    pairs = ((owner_hbm, owner_ref), (dest_hbm, dest_ref), (len_hbm, len_ref), (keys_hbm, keys), (values_hbm, values))
    loads = [pltpu.make_async_copy(a, b, sems.at[i]) for i, (a, b) in enumerate(pairs)]
    for load in loads:
        load.start()
    zeros = jnp.zeros((width, HD), jnp.bfloat16)
    for b in range(blocks):
        out_ref[b, width : 2 * width, :] = zeros
        out_ref[b, 3 * width : 4 * width, :] = zeros
    bits = half.bit_length() - 1
    my_half = lax.axis_index("pool") >> bits
    for i in range(2 * half):
        count[i] = 0
    for i in range(blocks * 2 * CAP):
        length[i] = 0
        target[i] = 0
    for load in loads[:3]:
        load.wait()
    places = []
    for p in range(prompts):
        group = owner_ref[p]
        rank = jnp.minimum(count[group], CAP - 1)
        count[group] = rank + 1
        block = group & (half - 1)
        other = (group >> bits) ^ my_half
        slot = block * (2 * CAP) + other * CAP + rank
        length[slot] = len_ref[p]
        target[slot] = dest_ref[p]
        places.append((block, other * 2 * width + rank * plen))
    row = lax.broadcasted_iota(jnp.int32, (16, 128), 0)
    lane = lax.broadcasted_iota(jnp.int32, (16, 128), 1)
    pos = lane % plen
    second = (lane // plen) % CAP == 1
    lower = row < 8
    for b in range(blocks):
        s = b * 2 * CAP
        limit = jnp.where(
            lower,
            jnp.where(second, length[s + 1], length[s]),
            jnp.where(second, length[s + 3], length[s + 2]),
        )
        code = jnp.where(
            lower,
            jnp.where(second, target[s + 1], target[s]),
            jnp.where(second, target[s + 3], target[s + 2]),
        )
        code = jnp.where(pos < limit, code, -1)
        out_ref[b, 4 * width :, :] = code.astype(jnp.float32).astype(jnp.bfloat16)
    for load in loads[3:]:
        load.wait()
    for p, (block, at) in enumerate(places):
        out_ref[block, pl.ds(pl.multiple_of(at, plen), plen), :] = keys[p]
        out_ref[block, pl.ds(pl.multiple_of(at + width, plen), plen), :] = values[p]


def split_heads(q_ref, scratch):
    seqs = q_ref.shape[0]
    heads = q_ref.shape[1] // HD
    for h in range(heads):
        scratch[h * seqs : (h + 1) * seqs, :] = q_ref[:, h * HD : (h + 1) * HD].astype(jnp.float32)
    return [scratch[pl.ds(s, heads, stride=seqs), :] for s in range(seqs)]


def group(ref, b, at, width):
    return jnp.concatenate([ref[b + i, at : at + width, :] for i in range(GROUP)], axis=0)


def prompt_scores(q, got_ref, other, scale):
    blocks, rows, _ = got_ref.shape
    width = (rows - 16) // 4
    seq = lax.broadcasted_iota(jnp.int32, (q.shape[0], 128), 0) // 8
    left = lax.broadcasted_iota(jnp.int32, (1, 128), 1) < width
    out = []
    for b in range(0, blocks, GROUP):
        keys = group(got_ref, b, other * 2 * width, width)
        s = lax.dot_general(q, keys, NT, preferred_element_type=jnp.float32) * scale
        for i in range(0, GROUP, 2):
            meta = [got_ref[b + i + k, 4 * width :, :].astype(jnp.float32)[other * 8 : other * 8 + 1] for k in range(2)]
            code = jnp.where(left, meta[0], meta[1]).astype(jnp.int32)
            out.append(jnp.where(seq == code, s[:, i * width : (i + 2) * width], NEG))
    return out


def prompt_sum(weights, got_ref, other):
    blocks, rows, _ = got_ref.shape
    width = (rows - 16) // 4
    step = GROUP // 2
    total = None
    for i in range(0, len(weights), step):
        values = group(got_ref, 2 * i, other * 2 * width + width, width)
        part = jnp.concatenate([w.astype(jnp.bfloat16) for w in weights[i : i + step]], axis=1)
        part = jnp.dot(part, values, preferred_element_type=jnp.float32)
        total = part if total is None else total + part
    return total


def partner_kernel(scale, q_ref, got_ref, out_ref, scratch):
    q = jnp.concatenate(split_heads(q_ref, scratch), axis=0).astype(jnp.bfloat16)
    scores = prompt_scores(q, got_ref, 1, scale)
    top = functools.reduce(jnp.maximum, scores)
    top = jnp.max(top, axis=1, keepdims=True).astype(jnp.bfloat16).astype(jnp.float32)
    exps = [jnp.exp(s - top) for s in scores]
    total = jnp.sum(functools.reduce(jnp.add, exps), axis=1, keepdims=True)
    rows = q.shape[0]
    out_ref[:rows, :] = prompt_sum(exps, got_ref, 1).astype(jnp.bfloat16)
    high = total.astype(jnp.bfloat16).astype(jnp.float32)
    lane = lax.broadcasted_iota(jnp.int32, (rows, 128), 1)
    stats = jnp.where(lane == 0, top, jnp.where(lane == 1, high, total - high))
    out_ref[rows:, :] = jnp.transpose(stats)[:16, :].astype(jnp.bfloat16)


def cache_kernel(scale, lens_ref, q_ref, keys_ref, values_ref, weight_hbm, out_ref, top_ref, sum_ref, q_out_ref, weight_ref, scratch, sem):
    load = pltpu.make_async_copy(weight_hbm.at[:EARLY], weight_ref, sem)
    load.start()
    seqs, ctx, _ = keys_ref.shape
    rows = split_heads(q_ref, scratch)
    q_out_ref[...] = jnp.concatenate(rows, axis=0)
    heads = rows[0].shape[0]
    col = lax.broadcasted_iota(jnp.int32, (heads, ctx), 1)
    scores = []
    for s in range(seqs):
        sc = lax.dot_general(rows[s].astype(jnp.bfloat16), keys_ref[s], NT, preferred_element_type=jnp.float32)
        scores.append(jnp.where(col < lens_ref[s], sc * scale, NEG))
    scores = jnp.concatenate(scores, axis=0)
    top = jnp.max(scores, axis=1, keepdims=True)
    exps = jnp.exp(scores - top)
    total = jnp.sum(exps, axis=1, keepdims=True)
    for s in range(seqs):
        w = exps[s * heads : (s + 1) * heads].astype(jnp.bfloat16)
        out_ref[s * heads : (s + 1) * heads, :] = jnp.dot(w, values_ref[s], preferred_element_type=jnp.float32)
    top_ref[...] = jnp.broadcast_to(top, top_ref.shape)
    sum_ref[...] = jnp.broadcast_to(total, sum_ref.shape)
    load.wait()


def own_kernel(scale, q_ref, got_ref, cache_ref, cache_top_ref, cache_sum_ref, weight_hbm, out_ref, top_ref, sum_ref, weight_ref, late_ref, sem, sems):
    load = pltpu.make_async_copy(weight_hbm.at[EARLY : weight_hbm.shape[0] - LATE], weight_ref, sem)
    load.start()
    x = lax.axis_index("tensor") >> 1
    loads = late_loads([x ^ 1, x ^ 2], weight_hbm, late_ref, sems)
    scores = prompt_scores(q_ref[...].astype(jnp.bfloat16), got_ref, 0, scale)
    top = jnp.max(functools.reduce(jnp.maximum, scores), axis=1, keepdims=True)
    top = jnp.maximum(top, cache_top_ref[...])
    exps = [jnp.exp(s - top) for s in scores]
    total = jnp.sum(functools.reduce(jnp.add, exps), axis=1, keepdims=True)
    near = jnp.exp(cache_top_ref[...] - top)
    out_ref[...] = prompt_sum(exps, got_ref, 0) + cache_ref[...] * near
    top_ref[...] = top
    sum_ref[...] = total + cache_sum_ref[...] * near
    for copy in [load] + loads:
        copy.wait()


def late_loads(places, weight_hbm, late_ref, sems):
    cols = late_ref.shape[2]
    rows = pl.ds(weight_hbm.shape[0] - LATE, LATE)
    loads = []
    for k, place in enumerate(places):
        at = pl.ds(pl.multiple_of(place * cols, cols), cols)
        loads.append(pltpu.make_async_copy(weight_hbm.at[rows, at], late_ref.at[k], sems.at[k]))
        loads[-1].start()
    return loads


def columns(attended, places, weights, late_ref, loads, out_ref):
    cols = late_ref.shape[2]
    step = cols // 2
    parts = []
    for place in places:
        for h in range(2):
            span = pl.ds(pl.multiple_of(place * cols + h * step, step), step)
            part, at = 0.0, 0
            for ref in weights:
                depth = ref.shape[0]
                part += jnp.dot(attended[:, at : at + depth], ref[:, span], preferred_element_type=jnp.float32)
                at += depth
            parts.append(part)
    for k in range(len(places)):
        if loads:
            loads[k].wait()
        for h in range(2):
            span = slice(h * step, (h + 1) * step)
            part = jnp.dot(attended[:, -LATE:], late_ref[k, :, span], preferred_element_type=jnp.float32)
            out_ref[k, :, span] = (parts[2 * k + h] + part).astype(out_ref.dtype)


def send_kernel(main_ref, top_ref, sum_ref, back_ref, weight0_ref, weight1_ref, late_ref, attended_ref, out_ref, scratch):
    x = lax.axis_index("tensor") >> 1
    places = [x ^ 1, x ^ 2]
    seqs = attended_ref.shape[0]
    rows = main_ref.shape[0]
    heads = rows // seqs
    stats = jnp.concatenate([back_ref[rows:, :].astype(jnp.float32)] * (128 // 16), axis=0)
    stats = jnp.transpose(stats)
    far_top = stats[:, 0:1]
    far_sum = stats[:, 1:2] + stats[:, 2:3]
    top = jnp.maximum(top_ref[...], far_top)
    near = jnp.exp(top_ref[...] - top)
    far = jnp.exp(far_top - top)
    total = sum_ref[...] * near + far_sum * far
    scratch[...] = (main_ref[...] * near + back_ref[:rows, :].astype(jnp.float32) * far) / total
    attended = jnp.concatenate(
        [scratch[pl.ds(h, seqs, stride=heads), :].astype(jnp.bfloat16) for h in range(heads)], axis=1
    )
    attended_ref[...] = attended
    columns(attended, places, (weight0_ref, weight1_ref), late_ref, [], out_ref)


def keep_kernel(attended_ref, weight0_ref, weight1_ref, weight_hbm, out_ref, late_ref, sems):
    x = lax.axis_index("tensor") >> 1
    places = [x, x ^ 3]
    loads = late_loads(places, weight_hbm, late_ref, sems)
    columns(attended_ref[...], places, (weight0_ref, weight1_ref), late_ref, loads, out_ref)


def vmem(n):
    return [pl.BlockSpec(memory_space=VMEM)] * n


def smem(n):
    return [pl.BlockSpec(memory_space=SMEM)] * n


def shards(
    queries,
    cache_keys,
    cache_values,
    context_lens,
    prompt_keys,
    prompt_values,
    prompt_lens,
    matching,
    dest_seq,
    out_weight,
):
    seqs, q_width = queries.shape
    ctx = cache_keys.shape[1]
    prompts, plen, _ = prompt_keys.shape
    pool = lax.axis_size("pool")
    pieces = lax.axis_size("tensor")
    out_cols = out_weight.shape[1]
    half = pool // 2
    rows = q_width // HD * seqs
    width = CAP * plen
    scale = 1.0 / math.sqrt(HD)
    swap = [(i, (i + half) % pool) for i in range(pool)]
    halves = [list(range(half)), list(range(half, pool))]
    in_hbm = lambda x: pltpu.with_memory_space_constraint(x, pltpu.HBM)
    anywhere = pl.BlockSpec(memory_space=pltpu.HBM)
    small = VMEM((rows, HD), jnp.float32)
    far_queries = lax.ppermute(queries, "pool", swap)
    packed = pl.pallas_call(
        functools.partial(pack_kernel, half),
        out_shape=jax.ShapeDtypeStruct((half, 4 * width + 16, HD), jnp.bfloat16),
        in_specs=[anywhere] * 5,
        out_specs=pl.BlockSpec(memory_space=VMEM),
        scratch_shapes=[SMEM((prompts,), jnp.int32)] * 3
        + [VMEM((prompts, plen, HD), jnp.bfloat16)] * 2
        + [pltpu.SemaphoreType.DMA((5,)), SMEM((pool,), jnp.int32)]
        + [SMEM((half * 2 * CAP,), jnp.int32)] * 2,
        compiler_params=pltpu.CompilerParams(vmem_limit_bytes=16 << 20),
        name="pack",
    )(*[in_hbm(x) for x in (matching.reshape(-1), dest_seq, prompt_lens, prompt_keys, prompt_values)])
    got = lax.all_to_all(packed, "pool", 0, 0, axis_index_groups=halves)
    cache, cache_top, cache_sum, heads_first, weight0 = pl.pallas_call(
        functools.partial(cache_kernel, scale),
        out_shape=[jax.ShapeDtypeStruct((rows, HD), jnp.float32)] * 4 + [VMEM((EARLY, out_cols), out_weight.dtype)],
        in_specs=smem(1) + vmem(3) + [anywhere],
        out_specs=vmem(5),
        scratch_shapes=[small, pltpu.SemaphoreType.DMA],
        compiler_params=pltpu.CompilerParams(vmem_limit_bytes=24 << 20),
        cost_estimate=pl.CostEstimate(flops=200_000_000, bytes_accessed=12_000_000, transcendentals=200_000),
        name="cache",
    )(*[in_hbm(x) for x in (context_lens, queries, cache_keys, cache_values, out_weight)])
    far_queries, cache = lax.optimization_barrier((far_queries, cache))
    back = pl.pallas_call(
        functools.partial(partner_kernel, scale),
        out_shape=jax.ShapeDtypeStruct((rows + 16, HD), jnp.bfloat16),
        in_specs=vmem(2),
        out_specs=pl.BlockSpec(memory_space=VMEM),
        scratch_shapes=[small],
        compiler_params=pltpu.CompilerParams(vmem_limit_bytes=16 << 20),
        name="partner",
    )(far_queries, got)
    back = lax.ppermute(back, "pool", swap)
    wide = out_cols // pieces * 2
    main, top, total, weight, late_send = pl.pallas_call(
        functools.partial(own_kernel, scale),
        out_shape=[jax.ShapeDtypeStruct((rows, HD), jnp.float32)] * 3 + [VMEM((out_weight.shape[0] - EARLY - LATE, out_cols), out_weight.dtype)]
        + [VMEM((2, LATE, wide), out_weight.dtype)],
        in_specs=vmem(5) + [anywhere],
        out_specs=vmem(5),
        scratch_shapes=[pltpu.SemaphoreType.DMA, pltpu.SemaphoreType.DMA((2,))],
        compiler_params=pltpu.CompilerParams(vmem_limit_bytes=16 << 20),
        cost_estimate=pl.CostEstimate(flops=100_000_000, bytes_accessed=2_000_000, transcendentals=200_000),
        name="own",
    )(heads_first, got, cache, cache_top, cache_sum, in_hbm(out_weight))
    pairs = jax.ShapeDtypeStruct((2, seqs, wide), jnp.bfloat16)
    late = [VMEM((2, LATE, wide), out_weight.dtype), pltpu.SemaphoreType.DMA((2,))]
    attended, send = pl.pallas_call(
        send_kernel,
        out_shape=[jax.ShapeDtypeStruct((seqs, q_width), jnp.bfloat16), pairs],
        in_specs=vmem(7),
        out_specs=vmem(2),
        scratch_shapes=[small],
        compiler_params=pltpu.CompilerParams(vmem_limit_bytes=13 << 20),
        name="send",
    )(main, top, total, back, weight0, weight, late_send)
    keep = pl.pallas_call(
        keep_kernel,
        out_shape=pairs,
        in_specs=vmem(3) + [anywhere],
        out_specs=pl.BlockSpec(memory_space=VMEM),
        scratch_shapes=late,
        compiler_params=pltpu.CompilerParams(vmem_limit_bytes=13 << 20),
        cost_estimate=pl.CostEstimate(flops=8_000_000_000, bytes_accessed=16_000_000, transcendentals=0),
        name="keep",
    )(attended, weight0, weight, in_hbm(out_weight))
    second = lax.axis_index("tensor") % 2 == 1
    keep, second = lax.optimization_barrier((keep, second))

    def trade(x, partner):
        return lax.ppermute(x, "tensor", [(2 * i + k, 2 * partner(i) + k) for i in range(pieces // 2) for k in range(2)])

    sums = keep.astype(jnp.float32) + trade(send, lambda i: i ^ 1).astype(jnp.float32)
    sums = sums[0] + trade(sums[1].astype(jnp.bfloat16), lambda i: 3 - i).astype(jnp.float32)
    halves = jnp.split(sums, 2, axis=1)
    away = jnp.where(second, halves[0], halves[1]).astype(jnp.bfloat16)
    near = jnp.where(second, halves[1], halves[0])
    away = lax.ppermute(away, "tensor", [(i, i ^ 1) for i in range(pieces)])
    return (near + away.astype(jnp.float32)).astype(jnp.bfloat16)


def solution(mesh):
    placed = (
        P("pool", "tensor"),
        P("pool", None, "tensor"),
        P("pool", None, "tensor"),
        P("pool"),
        P("pool", None, "tensor"),
        P("pool", None, "tensor"),
        P("pool"),
        P("pool", None),
        P("pool"),
        P("tensor", None),
    )
    return jax.shard_map(
        shards, mesh=mesh, in_specs=placed, out_specs=P("pool", "tensor"), check_vma=False
    )
```

```python
import functools
import math

import jax
import jax.numpy as jnp
from jax import lax
from jax.experimental import pallas as pl
from jax.experimental.pallas import tpu as pltpu
from jax.sharding import PartitionSpec as P

HD = 128
CAP = 2
GROUP = 4
EARLY = 256
LATE = 512
NEG = -(2.0**99)
VMEM = pltpu.VMEM
SMEM = pltpu.SMEM
NT = (((1,), (1,)), ((), ()))


def pack_kernel(
    half, owner_hbm, dest_hbm, len_hbm, keys_hbm, values_hbm, out_ref, owner_ref, dest_ref, len_ref, keys, values, sems, count, length, target
):
    prompts, plen, _ = keys.shape
    blocks = out_ref.shape[0]
    width = CAP * plen
    pairs = ((owner_hbm, owner_ref), (dest_hbm, dest_ref), (len_hbm, len_ref), (keys_hbm, keys), (values_hbm, values))
    loads = [pltpu.make_async_copy(a, b, sems.at[i]) for i, (a, b) in enumerate(pairs)]
    for load in loads:
        load.start()
    zeros = jnp.zeros((width, HD), jnp.bfloat16)
    for b in range(blocks):
        out_ref[b, width : 2 * width, :] = zeros
        out_ref[b, 3 * width : 4 * width, :] = zeros
    bits = half.bit_length() - 1
    my_half = lax.axis_index("pool") >> bits
    for i in range(2 * half):
        count[i] = 0
    for i in range(blocks * 2 * CAP):
        length[i] = 0
        target[i] = 0
    for load in loads[:3]:
        load.wait()
    places = []
    for p in range(prompts):
        group = owner_ref[p]
        rank = jnp.minimum(count[group], CAP - 1)
        count[group] = rank + 1
        block = group & (half - 1)
        other = (group >> bits) ^ my_half
        slot = block * (2 * CAP) + other * CAP + rank
        length[slot] = len_ref[p]
        target[slot] = dest_ref[p]
        places.append((block, other * 2 * width + rank * plen))
    row = lax.broadcasted_iota(jnp.int32, (16, 128), 0)
    lane = lax.broadcasted_iota(jnp.int32, (16, 128), 1)
    pos = lane % plen
    second = (lane // plen) % CAP == 1
    lower = row < 8
    for b in range(blocks):
        s = b * 2 * CAP
        limit = jnp.where(
            lower,
            jnp.where(second, length[s + 1], length[s]),
            jnp.where(second, length[s + 3], length[s + 2]),
        )
        code = jnp.where(
            lower,
            jnp.where(second, target[s + 1], target[s]),
            jnp.where(second, target[s + 3], target[s + 2]),
        )
        code = jnp.where(pos < limit, code, -1)
        out_ref[b, 4 * width :, :] = code.astype(jnp.float32).astype(jnp.bfloat16)
    for load in loads[3:]:
        load.wait()
    for p, (block, at) in enumerate(places):
        out_ref[block, pl.ds(pl.multiple_of(at, plen), plen), :] = keys[p]
        out_ref[block, pl.ds(pl.multiple_of(at + width, plen), plen), :] = values[p]


def split_heads(q_ref, scratch):
    seqs = q_ref.shape[0]
    heads = q_ref.shape[1] // HD
    for h in range(heads):
        scratch[h * seqs : (h + 1) * seqs, :] = q_ref[:, h * HD : (h + 1) * HD].astype(jnp.float32)
    return [scratch[pl.ds(s, heads, stride=seqs), :] for s in range(seqs)]


def group(ref, b, at, width):
    return jnp.concatenate([ref[b + i, at : at + width, :] for i in range(GROUP)], axis=0)


def prompt_scores(q, got_ref, other, scale):
    blocks, rows, _ = got_ref.shape
    width = (rows - 16) // 4
    seq = lax.broadcasted_iota(jnp.int32, (q.shape[0], 128), 0) // 8
    left = lax.broadcasted_iota(jnp.int32, (1, 128), 1) < width
    out = []
    for b in range(0, blocks, GROUP):
        keys = group(got_ref, b, other * 2 * width, width)
        s = lax.dot_general(q, keys, NT, preferred_element_type=jnp.float32) * scale
        for i in range(0, GROUP, 2):
            meta = [got_ref[b + i + k, 4 * width :, :].astype(jnp.float32)[other * 8 : other * 8 + 1] for k in range(2)]
            code = jnp.where(left, meta[0], meta[1]).astype(jnp.int32)
            out.append(jnp.where(seq == code, s[:, i * width : (i + 2) * width], NEG))
    return out


def prompt_sum(weights, got_ref, other):
    blocks, rows, _ = got_ref.shape
    width = (rows - 16) // 4
    step = GROUP // 2
    total = None
    for i in range(0, len(weights), step):
        values = group(got_ref, 2 * i, other * 2 * width + width, width)
        part = jnp.concatenate([w.astype(jnp.bfloat16) for w in weights[i : i + step]], axis=1)
        part = jnp.dot(part, values, preferred_element_type=jnp.float32)
        total = part if total is None else total + part
    return total


def partner_kernel(scale, q_ref, got_ref, out_ref, scratch):
    q = jnp.concatenate(split_heads(q_ref, scratch), axis=0).astype(jnp.bfloat16)
    scores = prompt_scores(q, got_ref, 1, scale)
    top = functools.reduce(jnp.maximum, scores)
    top = jnp.max(top, axis=1, keepdims=True).astype(jnp.bfloat16).astype(jnp.float32)
    exps = [jnp.exp(s - top) for s in scores]
    total = jnp.sum(functools.reduce(jnp.add, exps), axis=1, keepdims=True)
    rows = q.shape[0]
    out_ref[:rows, :] = prompt_sum(exps, got_ref, 1).astype(jnp.bfloat16)
    high = total.astype(jnp.bfloat16).astype(jnp.float32)
    lane = lax.broadcasted_iota(jnp.int32, (rows, 128), 1)
    stats = jnp.where(lane == 0, top, jnp.where(lane == 1, high, total - high))
    out_ref[rows:, :] = jnp.transpose(stats)[:16, :].astype(jnp.bfloat16)


def cache_kernel(scale, lens_ref, q_ref, keys_ref, values_ref, weight_hbm, out_ref, top_ref, sum_ref, q_out_ref, weight_ref, scratch, sem):
    load = pltpu.make_async_copy(weight_hbm.at[:EARLY], weight_ref, sem)
    load.start()
    seqs, ctx, _ = keys_ref.shape
    rows = split_heads(q_ref, scratch)
    q_out_ref[...] = jnp.concatenate(rows, axis=0)
    heads = rows[0].shape[0]
    col = lax.broadcasted_iota(jnp.int32, (heads, ctx), 1)
    scores = []
    for s in range(seqs):
        sc = lax.dot_general(rows[s].astype(jnp.bfloat16), keys_ref[s], NT, preferred_element_type=jnp.float32)
        scores.append(jnp.where(col < lens_ref[s], sc * scale, NEG))
    scores = jnp.concatenate(scores, axis=0)
    top = jnp.max(scores, axis=1, keepdims=True)
    exps = jnp.exp(scores - top)
    total = jnp.sum(exps, axis=1, keepdims=True)
    for s in range(seqs):
        w = exps[s * heads : (s + 1) * heads].astype(jnp.bfloat16)
        out_ref[s * heads : (s + 1) * heads, :] = jnp.dot(w, values_ref[s], preferred_element_type=jnp.float32)
    top_ref[...] = jnp.broadcast_to(top, top_ref.shape)
    sum_ref[...] = jnp.broadcast_to(total, sum_ref.shape)
    load.wait()


def own_kernel(scale, q_ref, got_ref, cache_ref, cache_top_ref, cache_sum_ref, weight_hbm, out_ref, top_ref, sum_ref, weight_ref, late_ref, sem, sems):
    load = pltpu.make_async_copy(weight_hbm.at[EARLY : weight_hbm.shape[0] - LATE], weight_ref, sem)
    load.start()
    x = lax.axis_index("tensor") >> 1
    loads = late_loads([x ^ 1, x ^ 2], weight_hbm, late_ref, sems)
    scores = prompt_scores(q_ref[...].astype(jnp.bfloat16), got_ref, 0, scale)
    top = jnp.max(functools.reduce(jnp.maximum, scores), axis=1, keepdims=True)
    top = jnp.maximum(top, cache_top_ref[...])
    exps = [jnp.exp(s - top) for s in scores]
    total = jnp.sum(functools.reduce(jnp.add, exps), axis=1, keepdims=True)
    near = jnp.exp(cache_top_ref[...] - top)
    out_ref[...] = prompt_sum(exps, got_ref, 0) + cache_ref[...] * near
    top_ref[...] = top
    sum_ref[...] = total + cache_sum_ref[...] * near
    for copy in [load] + loads:
        copy.wait()


def late_loads(places, weight_hbm, late_ref, sems):
    cols = late_ref.shape[2]
    rows = pl.ds(weight_hbm.shape[0] - LATE, LATE)
    loads = []
    for k, place in enumerate(places):
        at = pl.ds(pl.multiple_of(place * cols, cols), cols)
        loads.append(pltpu.make_async_copy(weight_hbm.at[rows, at], late_ref.at[k], sems.at[k]))
        loads[-1].start()
    return loads


def columns(attended, places, weights, late_ref, loads, out_ref):
    cols = late_ref.shape[2]
    step = cols // 2
    parts = []
    for place in places:
        for h in range(2):
            span = pl.ds(pl.multiple_of(place * cols + h * step, step), step)
            part, at = 0.0, 0
            for ref in weights:
                depth = ref.shape[0]
                part += jnp.dot(attended[:, at : at + depth], ref[:, span], preferred_element_type=jnp.float32)
                at += depth
            parts.append(part)
    for k in range(len(places)):
        if loads:
            loads[k].wait()
        for h in range(2):
            span = slice(h * step, (h + 1) * step)
            part = jnp.dot(attended[:, -LATE:], late_ref[k, :, span], preferred_element_type=jnp.float32)
            out_ref[k, :, span] = (parts[2 * k + h] + part).astype(out_ref.dtype)


def send_kernel(main_ref, top_ref, sum_ref, back_ref, weight0_ref, weight1_ref, late_ref, attended_ref, out_ref, scratch):
    x = lax.axis_index("tensor") >> 1
    places = [x ^ 1, x ^ 2]
    seqs = attended_ref.shape[0]
    rows = main_ref.shape[0]
    heads = rows // seqs
    stats = jnp.concatenate([back_ref[rows:, :].astype(jnp.float32)] * (128 // 16), axis=0)
    stats = jnp.transpose(stats)
    far_top = stats[:, 0:1]
    far_sum = stats[:, 1:2] + stats[:, 2:3]
    top = jnp.maximum(top_ref[...], far_top)
    near = jnp.exp(top_ref[...] - top)
    far = jnp.exp(far_top - top)
    total = sum_ref[...] * near + far_sum * far
    scratch[...] = (main_ref[...] * near + back_ref[:rows, :].astype(jnp.float32) * far) / total
    attended = jnp.concatenate(
        [scratch[pl.ds(h, seqs, stride=heads), :].astype(jnp.bfloat16) for h in range(heads)], axis=1
    )
    attended_ref[...] = attended
    columns(attended, places, (weight0_ref, weight1_ref), late_ref, [], out_ref)


def keep_kernel(attended_ref, weight0_ref, weight1_ref, weight_hbm, out_ref, late_ref, sems):
    x = lax.axis_index("tensor") >> 1
    places = [x, x ^ 3]
    loads = late_loads(places, weight_hbm, late_ref, sems)
    columns(attended_ref[...], places, (weight0_ref, weight1_ref), late_ref, loads, out_ref)


def vmem(n):
    return [pl.BlockSpec(memory_space=VMEM)] * n


def smem(n):
    return [pl.BlockSpec(memory_space=SMEM)] * n


def shards(
    queries,
    cache_keys,
    cache_values,
    context_lens,
    prompt_keys,
    prompt_values,
    prompt_lens,
    matching,
    dest_seq,
    out_weight,
):
    seqs, q_width = queries.shape
    ctx = cache_keys.shape[1]
    prompts, plen, _ = prompt_keys.shape
    pool = lax.axis_size("pool")
    pieces = lax.axis_size("tensor")
    out_cols = out_weight.shape[1]
    half = pool // 2
    rows = q_width // HD * seqs
    width = CAP * plen
    scale = 1.0 / math.sqrt(HD)
    swap = [(i, (i + half) % pool) for i in range(pool)]
    halves = [list(range(half)), list(range(half, pool))]
    in_hbm = lambda x: pltpu.with_memory_space_constraint(x, pltpu.HBM)
    anywhere = pl.BlockSpec(memory_space=pltpu.HBM)
    small = VMEM((rows, HD), jnp.float32)
    far_queries = lax.ppermute(queries, "pool", swap)
    packed = pl.pallas_call(
        functools.partial(pack_kernel, half),
        out_shape=jax.ShapeDtypeStruct((half, 4 * width + 16, HD), jnp.bfloat16),
        in_specs=[anywhere] * 5,
        out_specs=pl.BlockSpec(memory_space=VMEM),
        scratch_shapes=[SMEM((prompts,), jnp.int32)] * 3
        + [VMEM((prompts, plen, HD), jnp.bfloat16)] * 2
        + [pltpu.SemaphoreType.DMA((5,)), SMEM((pool,), jnp.int32)]
        + [SMEM((half * 2 * CAP,), jnp.int32)] * 2,
        compiler_params=pltpu.CompilerParams(vmem_limit_bytes=16 << 20),
        name="pack",
    )(*[in_hbm(x) for x in (matching.reshape(-1), dest_seq, prompt_lens, prompt_keys, prompt_values)])
    got = lax.all_to_all(packed, "pool", 0, 0, axis_index_groups=halves)
    cache, cache_top, cache_sum, heads_first, weight0 = pl.pallas_call(
        functools.partial(cache_kernel, scale),
        out_shape=[jax.ShapeDtypeStruct((rows, HD), jnp.float32)] * 4 + [VMEM((EARLY, out_cols), out_weight.dtype)],
        in_specs=smem(1) + vmem(3) + [anywhere],
        out_specs=vmem(5),
        scratch_shapes=[small, pltpu.SemaphoreType.DMA],
        compiler_params=pltpu.CompilerParams(vmem_limit_bytes=24 << 20),
        cost_estimate=pl.CostEstimate(flops=200_000_000, bytes_accessed=12_000_000, transcendentals=200_000),
        name="cache",
    )(*[in_hbm(x) for x in (context_lens, queries, cache_keys, cache_values, out_weight)])
    far_queries, cache = lax.optimization_barrier((far_queries, cache))
    back = pl.pallas_call(
        functools.partial(partner_kernel, scale),
        out_shape=jax.ShapeDtypeStruct((rows + 16, HD), jnp.bfloat16),
        in_specs=vmem(2),
        out_specs=pl.BlockSpec(memory_space=VMEM),
        scratch_shapes=[small],
        compiler_params=pltpu.CompilerParams(vmem_limit_bytes=16 << 20),
        name="partner",
    )(far_queries, got)
    back = lax.ppermute(back, "pool", swap)
    wide = out_cols // pieces * 2
    main, top, total, weight, late_send = pl.pallas_call(
        functools.partial(own_kernel, scale),
        out_shape=[jax.ShapeDtypeStruct((rows, HD), jnp.float32)] * 3 + [VMEM((out_weight.shape[0] - EARLY - LATE, out_cols), out_weight.dtype)]
        + [VMEM((2, LATE, wide), out_weight.dtype)],
        in_specs=vmem(5) + [anywhere],
        out_specs=vmem(5),
        scratch_shapes=[pltpu.SemaphoreType.DMA, pltpu.SemaphoreType.DMA((2,))],
        compiler_params=pltpu.CompilerParams(vmem_limit_bytes=16 << 20),
        cost_estimate=pl.CostEstimate(flops=100_000_000, bytes_accessed=2_000_000, transcendentals=200_000),
        name="own",
    )(heads_first, got, cache, cache_top, cache_sum, in_hbm(out_weight))
    pairs = jax.ShapeDtypeStruct((2, seqs, wide), jnp.bfloat16)
    late = [VMEM((2, LATE, wide), out_weight.dtype), pltpu.SemaphoreType.DMA((2,))]
    attended, send = pl.pallas_call(
        send_kernel,
        out_shape=[jax.ShapeDtypeStruct((seqs, q_width), jnp.bfloat16), pairs],
        in_specs=vmem(7),
        out_specs=vmem(2),
        scratch_shapes=[small],
        compiler_params=pltpu.CompilerParams(vmem_limit_bytes=13 << 20),
        name="send",
    )(main, top, total, back, weight0, weight, late_send)
    keep = pl.pallas_call(
        keep_kernel,
        out_shape=pairs,
        in_specs=vmem(3) + [anywhere],
        out_specs=pl.BlockSpec(memory_space=VMEM),
        scratch_shapes=late,
        compiler_params=pltpu.CompilerParams(vmem_limit_bytes=13 << 20),
        cost_estimate=pl.CostEstimate(flops=8_000_000_000, bytes_accessed=16_000_000, transcendentals=0),
        name="keep",
    )(attended, weight0, weight, in_hbm(out_weight))
    second = lax.axis_index("tensor") % 2 == 1
    keep, second = lax.optimization_barrier((keep, second))

    def trade(x, partner):
        return lax.ppermute(x, "tensor", [(2 * i + k, 2 * partner(i) + k) for i in range(pieces // 2) for k in range(2)])

    first = trade(send[1], lambda i: i ^ 1)
    later = trade(send[0], lambda i: i ^ 1)
    mirror = (keep[1].astype(jnp.float32) + first.astype(jnp.float32)).astype(jnp.bfloat16)
    mirror = trade(mirror, lambda i: 3 - i)
    sums = keep[0].astype(jnp.float32) + later.astype(jnp.float32) + mirror.astype(jnp.float32)
    halves = jnp.split(sums, 2, axis=1)
    away = jnp.where(second, halves[0], halves[1]).astype(jnp.bfloat16)
    near = jnp.where(second, halves[1], halves[0])
    away = lax.ppermute(away, "tensor", [(i, i ^ 1) for i in range(pieces)])
    return (near + away.astype(jnp.float32)).astype(jnp.bfloat16)


def solution(mesh):
    placed = (
        P("pool", "tensor"),
        P("pool", None, "tensor"),
        P("pool", None, "tensor"),
        P("pool"),
        P("pool", None, "tensor"),
        P("pool", None, "tensor"),
        P("pool"),
        P("pool", None),
        P("pool"),
        P("tensor", None),
    )
    return jax.shard_map(
        shards, mesh=mesh, in_specs=placed, out_specs=P("pool", "tensor"), check_vma=False
    )
```

```python
import functools
import math

import jax
import jax.numpy as jnp
from jax import lax
from jax.experimental import pallas as pl
from jax.experimental.pallas import tpu as pltpu
from jax.sharding import PartitionSpec as P

HD = 128
CAP = 2
GROUP = 4
EARLY = 256
LATE = 512
NEG = -(2.0**99)
VMEM = pltpu.VMEM
SMEM = pltpu.SMEM
NT = (((1,), (1,)), ((), ()))


def pack_kernel(
    half, owner_hbm, dest_hbm, len_hbm, keys_hbm, values_hbm, out_ref, owner_ref, dest_ref, len_ref, keys, values, sems, count, length, target
):
    prompts, plen, _ = keys.shape
    blocks = out_ref.shape[0]
    width = CAP * plen
    pairs = ((owner_hbm, owner_ref), (dest_hbm, dest_ref), (len_hbm, len_ref), (keys_hbm, keys), (values_hbm, values))
    loads = [pltpu.make_async_copy(a, b, sems.at[i]) for i, (a, b) in enumerate(pairs)]
    for load in loads:
        load.start()
    zeros = jnp.zeros((width, HD), jnp.bfloat16)
    for b in range(blocks):
        out_ref[b, width : 2 * width, :] = zeros
        out_ref[b, 3 * width : 4 * width, :] = zeros
    bits = half.bit_length() - 1
    my_half = lax.axis_index("pool") >> bits
    for i in range(2 * half):
        count[i] = 0
    for i in range(blocks * 2 * CAP):
        length[i] = 0
        target[i] = 0
    for load in loads[:3]:
        load.wait()
    places = []
    for p in range(prompts):
        group = owner_ref[p]
        rank = jnp.minimum(count[group], CAP - 1)
        count[group] = rank + 1
        block = group & (half - 1)
        other = (group >> bits) ^ my_half
        slot = block * (2 * CAP) + other * CAP + rank
        length[slot] = len_ref[p]
        target[slot] = dest_ref[p]
        places.append((block, other * 2 * width + rank * plen))
    row = lax.broadcasted_iota(jnp.int32, (16, 128), 0)
    lane = lax.broadcasted_iota(jnp.int32, (16, 128), 1)
    pos = lane % plen
    second = (lane // plen) % CAP == 1
    lower = row < 8
    for b in range(blocks):
        s = b * 2 * CAP
        limit = jnp.where(
            lower,
            jnp.where(second, length[s + 1], length[s]),
            jnp.where(second, length[s + 3], length[s + 2]),
        )
        code = jnp.where(
            lower,
            jnp.where(second, target[s + 1], target[s]),
            jnp.where(second, target[s + 3], target[s + 2]),
        )
        code = jnp.where(pos < limit, code, -1)
        out_ref[b, 4 * width :, :] = code.astype(jnp.float32).astype(jnp.bfloat16)
    for load in loads[3:]:
        load.wait()
    for p, (block, at) in enumerate(places):
        out_ref[block, pl.ds(pl.multiple_of(at, plen), plen), :] = keys[p]
        out_ref[block, pl.ds(pl.multiple_of(at + width, plen), plen), :] = values[p]


def split_heads(q_ref, scratch):
    seqs = q_ref.shape[0]
    heads = q_ref.shape[1] // HD
    for h in range(heads):
        scratch[h * seqs : (h + 1) * seqs, :] = q_ref[:, h * HD : (h + 1) * HD].astype(jnp.float32)
    return [scratch[pl.ds(s, heads, stride=seqs), :] for s in range(seqs)]


def group(ref, b, at, width):
    return jnp.concatenate([ref[b + i, at : at + width, :] for i in range(GROUP)], axis=0)


def prompt_scores(q, got_ref, other, scale):
    blocks, rows, _ = got_ref.shape
    width = (rows - 16) // 4
    seq = lax.broadcasted_iota(jnp.int32, (q.shape[0], 128), 0) // 8
    left = lax.broadcasted_iota(jnp.int32, (1, 128), 1) < width
    out = []
    for b in range(0, blocks, GROUP):
        keys = group(got_ref, b, other * 2 * width, width)
        s = lax.dot_general(q, keys, NT, preferred_element_type=jnp.float32) * scale
        for i in range(0, GROUP, 2):
            meta = [got_ref[b + i + k, 4 * width :, :].astype(jnp.float32)[other * 8 : other * 8 + 1] for k in range(2)]
            code = jnp.where(left, meta[0], meta[1]).astype(jnp.int32)
            out.append(jnp.where(seq == code, s[:, i * width : (i + 2) * width], NEG))
    return out


def prompt_sum(weights, got_ref, other):
    blocks, rows, _ = got_ref.shape
    width = (rows - 16) // 4
    step = GROUP // 2
    total = None
    for i in range(0, len(weights), step):
        values = group(got_ref, 2 * i, other * 2 * width + width, width)
        part = jnp.concatenate([w.astype(jnp.bfloat16) for w in weights[i : i + step]], axis=1)
        part = jnp.dot(part, values, preferred_element_type=jnp.float32)
        total = part if total is None else total + part
    return total


def partner_kernel(scale, q_ref, got_ref, out_ref, scratch):
    q = jnp.concatenate(split_heads(q_ref, scratch), axis=0).astype(jnp.bfloat16)
    scores = prompt_scores(q, got_ref, 1, scale)
    top = functools.reduce(jnp.maximum, scores)
    top = jnp.max(top, axis=1, keepdims=True).astype(jnp.bfloat16).astype(jnp.float32)
    exps = [jnp.exp(s - top) for s in scores]
    total = jnp.sum(functools.reduce(jnp.add, exps), axis=1, keepdims=True)
    rows = q.shape[0]
    out_ref[:rows, :] = prompt_sum(exps, got_ref, 1).astype(jnp.bfloat16)
    high = total.astype(jnp.bfloat16).astype(jnp.float32)
    lane = lax.broadcasted_iota(jnp.int32, (rows, 128), 1)
    stats = jnp.where(lane == 0, top, jnp.where(lane == 1, high, total - high))
    out_ref[rows:, :] = jnp.transpose(stats)[:16, :].astype(jnp.bfloat16)


def cache_kernel(scale, lens_ref, q_ref, keys_ref, values_ref, weight_hbm, out_ref, top_ref, sum_ref, q_out_ref, weight_ref, scratch, sem):
    load = pltpu.make_async_copy(weight_hbm.at[:EARLY], weight_ref, sem)
    load.start()
    seqs, ctx, _ = keys_ref.shape
    rows = split_heads(q_ref, scratch)
    q_out_ref[...] = jnp.concatenate(rows, axis=0)
    heads = rows[0].shape[0]
    col = lax.broadcasted_iota(jnp.int32, (heads, ctx), 1)
    scores = []
    for s in range(seqs):
        sc = lax.dot_general(rows[s].astype(jnp.bfloat16), keys_ref[s], NT, preferred_element_type=jnp.float32)
        scores.append(jnp.where(col < lens_ref[s], sc * scale, NEG))
    scores = jnp.concatenate(scores, axis=0)
    top = jnp.max(scores, axis=1, keepdims=True)
    exps = jnp.exp(scores - top)
    total = jnp.sum(exps, axis=1, keepdims=True)
    for s in range(seqs):
        w = exps[s * heads : (s + 1) * heads].astype(jnp.bfloat16)
        out_ref[s * heads : (s + 1) * heads, :] = jnp.dot(w, values_ref[s], preferred_element_type=jnp.float32)
    top_ref[...] = jnp.broadcast_to(top, top_ref.shape)
    sum_ref[...] = jnp.broadcast_to(total, sum_ref.shape)
    load.wait()


def own_kernel(scale, q_ref, got_ref, cache_ref, cache_top_ref, cache_sum_ref, weight_hbm, out_ref, top_ref, sum_ref, weight_ref, late_ref, sem, sems):
    load = pltpu.make_async_copy(weight_hbm.at[EARLY : weight_hbm.shape[0] - LATE], weight_ref, sem)
    load.start()
    x = lax.axis_index("tensor") >> 1
    loads = late_loads([x ^ 1, x ^ 2], weight_hbm, late_ref, sems)
    scores = prompt_scores(q_ref[...].astype(jnp.bfloat16), got_ref, 0, scale)
    top = jnp.max(functools.reduce(jnp.maximum, scores), axis=1, keepdims=True)
    top = jnp.maximum(top, cache_top_ref[...])
    exps = [jnp.exp(s - top) for s in scores]
    total = jnp.sum(functools.reduce(jnp.add, exps), axis=1, keepdims=True)
    near = jnp.exp(cache_top_ref[...] - top)
    out_ref[...] = prompt_sum(exps, got_ref, 0) + cache_ref[...] * near
    top_ref[...] = top
    sum_ref[...] = total + cache_sum_ref[...] * near
    for copy in [load] + loads:
        copy.wait()


def late_loads(places, weight_hbm, late_ref, sems):
    cols = late_ref.shape[2]
    rows = pl.ds(weight_hbm.shape[0] - LATE, LATE)
    loads = []
    for k, place in enumerate(places):
        at = pl.ds(pl.multiple_of(place * cols, cols), cols)
        loads.append(pltpu.make_async_copy(weight_hbm.at[rows, at], late_ref.at[k], sems.at[k]))
        loads[-1].start()
    return loads


def columns(attended, places, weights, late_ref, loads, out_ref):
    cols = late_ref.shape[2]
    step = cols // 2
    parts = []
    for place in places:
        for h in range(2):
            span = pl.ds(pl.multiple_of(place * cols + h * step, step), step)
            part, at = 0.0, 0
            for ref in weights:
                depth = ref.shape[0]
                part += jnp.dot(attended[:, at : at + depth], ref[:, span], preferred_element_type=jnp.float32)
                at += depth
            parts.append(part)
    for k in range(len(places)):
        if loads:
            loads[k].wait()
        for h in range(2):
            span = slice(h * step, (h + 1) * step)
            part = jnp.dot(attended[:, -LATE:], late_ref[k, :, span], preferred_element_type=jnp.float32)
            out_ref[k, :, span] = (parts[2 * k + h] + part).astype(out_ref.dtype)


def send_kernel(main_ref, top_ref, sum_ref, back_ref, weight0_ref, weight1_ref, late_ref, attended_ref, out_ref, scratch):
    x = lax.axis_index("tensor") >> 1
    places = [x ^ 1, x ^ 2]
    seqs = attended_ref.shape[0]
    rows = main_ref.shape[0]
    heads = rows // seqs
    stats = jnp.concatenate([back_ref[rows:, :].astype(jnp.float32)] * (128 // 16), axis=0)
    stats = jnp.transpose(stats)
    far_top = stats[:, 0:1]
    far_sum = stats[:, 1:2] + stats[:, 2:3]
    top = jnp.maximum(top_ref[...], far_top)
    near = jnp.exp(top_ref[...] - top)
    far = jnp.exp(far_top - top)
    total = sum_ref[...] * near + far_sum * far
    scratch[...] = (main_ref[...] * near + back_ref[:rows, :].astype(jnp.float32) * far) / total
    attended = jnp.concatenate(
        [scratch[pl.ds(h, seqs, stride=heads), :].astype(jnp.bfloat16) for h in range(heads)], axis=1
    )
    attended_ref[...] = attended
    columns(attended, places, (weight0_ref, weight1_ref), late_ref, [], out_ref)


def keep_kernel(attended_ref, weight0_ref, weight1_ref, weight_hbm, out_ref, late_ref, sems):
    x = lax.axis_index("tensor") >> 1
    places = [x, x ^ 3]
    loads = late_loads(places, weight_hbm, late_ref, sems)
    columns(attended_ref[...], places, (weight0_ref, weight1_ref), late_ref, loads, out_ref)


def vmem(n):
    return [pl.BlockSpec(memory_space=VMEM)] * n


def smem(n):
    return [pl.BlockSpec(memory_space=SMEM)] * n


def shards(
    queries,
    cache_keys,
    cache_values,
    context_lens,
    prompt_keys,
    prompt_values,
    prompt_lens,
    matching,
    dest_seq,
    out_weight,
):
    seqs, q_width = queries.shape
    ctx = cache_keys.shape[1]
    prompts, plen, _ = prompt_keys.shape
    pool = lax.axis_size("pool")
    pieces = lax.axis_size("tensor")
    out_cols = out_weight.shape[1]
    half = pool // 2
    rows = q_width // HD * seqs
    width = CAP * plen
    scale = 1.0 / math.sqrt(HD)
    swap = [(i, (i + half) % pool) for i in range(pool)]
    halves = [list(range(half)), list(range(half, pool))]
    in_hbm = lambda x: pltpu.with_memory_space_constraint(x, pltpu.HBM)
    anywhere = pl.BlockSpec(memory_space=pltpu.HBM)
    small = VMEM((rows, HD), jnp.float32)
    far_queries = lax.ppermute(queries, "pool", swap)
    packed = pl.pallas_call(
        functools.partial(pack_kernel, half),
        out_shape=jax.ShapeDtypeStruct((half, 4 * width + 16, HD), jnp.bfloat16),
        in_specs=[anywhere] * 5,
        out_specs=pl.BlockSpec(memory_space=VMEM),
        scratch_shapes=[SMEM((prompts,), jnp.int32)] * 3
        + [VMEM((prompts, plen, HD), jnp.bfloat16)] * 2
        + [pltpu.SemaphoreType.DMA((5,)), SMEM((pool,), jnp.int32)]
        + [SMEM((half * 2 * CAP,), jnp.int32)] * 2,
        compiler_params=pltpu.CompilerParams(vmem_limit_bytes=16 << 20),
        name="pack",
    )(*[in_hbm(x) for x in (matching.reshape(-1), dest_seq, prompt_lens, prompt_keys, prompt_values)])
    got = lax.all_to_all(packed, "pool", 0, 0, axis_index_groups=halves)
    cache, cache_top, cache_sum, heads_first, weight0 = pl.pallas_call(
        functools.partial(cache_kernel, scale),
        out_shape=[jax.ShapeDtypeStruct((rows, HD), jnp.float32)] * 4 + [VMEM((EARLY, out_cols), out_weight.dtype)],
        in_specs=smem(1) + vmem(3) + [anywhere],
        out_specs=vmem(5),
        scratch_shapes=[small, pltpu.SemaphoreType.DMA],
        compiler_params=pltpu.CompilerParams(vmem_limit_bytes=24 << 20),
        cost_estimate=pl.CostEstimate(flops=200_000_000, bytes_accessed=12_000_000, transcendentals=200_000),
        name="cache",
    )(*[in_hbm(x) for x in (context_lens, queries, cache_keys, cache_values, out_weight)])
    far_queries, cache = lax.optimization_barrier((far_queries, cache))
    back = pl.pallas_call(
        functools.partial(partner_kernel, scale),
        out_shape=jax.ShapeDtypeStruct((rows + 16, HD), jnp.bfloat16),
        in_specs=vmem(2),
        out_specs=pl.BlockSpec(memory_space=VMEM),
        scratch_shapes=[small],
        compiler_params=pltpu.CompilerParams(vmem_limit_bytes=16 << 20),
        name="partner",
    )(far_queries, got)
    back = lax.ppermute(back, "pool", swap)
    wide = out_cols // pieces * 2
    main, top, total, weight, late_send = pl.pallas_call(
        functools.partial(own_kernel, scale),
        out_shape=[jax.ShapeDtypeStruct((rows, HD), jnp.float32)] * 3 + [VMEM((out_weight.shape[0] - EARLY - LATE, out_cols), out_weight.dtype)]
        + [VMEM((2, LATE, wide), out_weight.dtype)],
        in_specs=vmem(5) + [anywhere],
        out_specs=vmem(5),
        scratch_shapes=[pltpu.SemaphoreType.DMA, pltpu.SemaphoreType.DMA((2,))],
        compiler_params=pltpu.CompilerParams(vmem_limit_bytes=16 << 20),
        cost_estimate=pl.CostEstimate(flops=100_000_000, bytes_accessed=2_000_000, transcendentals=200_000),
        name="own",
    )(heads_first, got, cache, cache_top, cache_sum, in_hbm(out_weight))
    pairs = jax.ShapeDtypeStruct((2, seqs, wide), jnp.bfloat16)
    late = [VMEM((2, LATE, wide), out_weight.dtype), pltpu.SemaphoreType.DMA((2,))]
    attended, send = pl.pallas_call(
        send_kernel,
        out_shape=[jax.ShapeDtypeStruct((seqs, q_width), jnp.bfloat16), pairs],
        in_specs=vmem(7),
        out_specs=vmem(2),
        scratch_shapes=[small],
        compiler_params=pltpu.CompilerParams(vmem_limit_bytes=13 << 20),
        name="send",
    )(main, top, total, back, weight0, weight, late_send)
    keep = pl.pallas_call(
        keep_kernel,
        out_shape=pairs,
        in_specs=vmem(3) + [anywhere],
        out_specs=pl.BlockSpec(memory_space=VMEM),
        scratch_shapes=late,
        compiler_params=pltpu.CompilerParams(vmem_limit_bytes=13 << 20),
        cost_estimate=pl.CostEstimate(flops=8_000_000_000, bytes_accessed=16_000_000, transcendentals=0),
        name="keep",
    )(attended, weight0, weight, in_hbm(out_weight))
    second = lax.axis_index("tensor") % 2 == 1
    keep, second = lax.optimization_barrier((keep, second))

    def trade(x, partner):
        return lax.ppermute(x, "tensor", [(2 * i + k, 2 * partner(i) + k) for i in range(pieces // 2) for k in range(2)])

    sums = keep.astype(jnp.float32) + trade(send, lambda i: i ^ 1).astype(jnp.float32)
    halves = jnp.split(sums, 2, axis=2)
    away = jnp.where(second, halves[0], halves[1]).astype(jnp.bfloat16)
    near = jnp.where(second, halves[1], halves[0])
    away = lax.ppermute(away, "tensor", [(i, i ^ 1) for i in range(pieces)])
    sums = near + away.astype(jnp.float32)
    other = trade(sums[1].astype(jnp.bfloat16), lambda i: 3 - i)
    return (sums[0] + other.astype(jnp.float32)).astype(jnp.bfloat16)


def solution(mesh):
    placed = (
        P("pool", "tensor"),
        P("pool", None, "tensor"),
        P("pool", None, "tensor"),
        P("pool"),
        P("pool", None, "tensor"),
        P("pool", None, "tensor"),
        P("pool"),
        P("pool", None),
        P("pool"),
        P("tensor", None),
    )
    return jax.shard_map(
        shards, mesh=mesh, in_specs=placed, out_specs=P("pool", "tensor"), check_vma=False
    )
```
